256 devices in a mesh: dp: 16 (over x, y), seq: 16 (over z, core).
Axes of the slice: x: 4, y: 4, z: 8, core: 2. Of those that a mesh axis runs over, the one named last changes fastest.
Arguments:
- queries: bfloat16 [16, 2048, 2048], P('dp', 'seq'), may hold values from -40 to 40
- keys: bfloat16 [16, 2048, 2048], P('dp', 'seq'), may hold values from -8 to 8
- values: bfloat16 [16, 2048, 2048], P('dp', 'seq'), may hold values from -6 to 6
- w_out: bfloat16 [2, 2048, 4096], P(None, None, 'seq'), may hold values from -0.125 to 0.125
- modality: int32 [16, 16], P('dp'), may hold values 0 or 1
- grad_out: bfloat16 [16, 2048, 4096], P('dp', 'seq'), may hold values from -6 to 6
Outputs:
- mixed: bfloat16 [16, 2048, 4096], P('dp', 'seq')
- grad_queries: bfloat16 [16, 2048, 2048], P('dp', 'seq')
- grad_keys: bfloat16 [16, 2048, 2048], P('dp', 'seq')
- grad_values: bfloat16 [16, 2048, 2048], P('dp', 'seq')
- grad_w_out: float32 [2, 2048, 4096], P(None, 'dp', 'seq')
The draws below stay inside these ranges and needn't reach their ends.
All inputs are finite; a program needn't handle non-finite values. No bound on the sum of `modality` on one device may be relied on, other than what follows from the above.
Results may differ from the reference program's by a relative error of at most 0.03.
Values may be sent and summed in bfloat16 or wider, within the bound.
A program may use at most 128 MiB of HBM per device.

```python
import jax
import jax.numpy as jnp
from jax import lax

D = 4096
HD = 128
BLOCK = 128
ROWS = 16
SEQ_LEN = 2048
NB = 16
HW = 2048
N_SEQ = 16


def shared_base(key):
    return jnp.clip(jax.random.normal(key, (ROWS, SEQ_LEN, HW), jnp.float32), -4.0, 4.0)


def draw_queries(key, part):
    key = jax.random.fold_in(key, 7)
    own_draw = jnp.clip(jax.random.normal(key, (ROWS, SEQ_LEN, HW), jnp.float32), -4.0, 4.0)
    return own_draw.astype(jnp.bfloat16)


def draw_keys(key, part):
    common = shared_base(key)
    return common.astype(jnp.bfloat16)


def place_ends(result, rng, smallest, largest):
    shape = result.shape
    index_at = [jax.random.randint(jax.random.fold_in(rng, axis), (), 0, shape[axis]) for axis in range(len(shape))]
    result = result.at[tuple(index_at)].set(smallest)
    longest = shape.index(max(shape))
    index_at[longest] = (index_at[longest] + 1) % shape[longest]
    return result.at[tuple(index_at)].set(largest)


def shard_levels(own_key, shape, pieces, low, largest):
    loudness, own = 1.0, jax.random.fold_in(own_key, 6)
    for axis_at, blocks in pieces:
        steps = jnp.exp(jax.random.uniform(jax.random.fold_in(own, axis_at), (blocks,), jnp.float32, low / len(pieces), largest / len(pieces)))
        loudness = loudness * jnp.repeat(steps, shape[axis_at] // blocks).reshape([-1 if axis == axis_at else 1 for axis in range(len(shape))])
    return loudness


def bell_draw(key, dims, deviation, limit, split=(), kind=jnp.bfloat16):
    entries = jax.random.normal(key, dims, jnp.float32) * deviation
    if len(split) > 0:
        entries = shard_levels(key, dims, split, -0.22, 0.18) * entries
    return jnp.clip(entries, min=-limit, max=limit).astype(kind)


def setup_inputs(seed: int = 0) -> dict:
    key_list = jax.random.split(jax.random.key(seed), 7)
    return {
        "queries": draw_queries(jax.random.fold_in(key_list[6], 71), 0),
        "keys": draw_keys(jax.random.fold_in(key_list[6], 71), 0),
        "values": bell_draw(key_list[2], (ROWS, SEQ_LEN, HW), 1.0, 6.0, ((0, 16), (1, 16))),
        "w_out": bell_draw(key_list[3], (2, HW, D), HW ** -0.5, 0.125, ((2, 16),)),
        "modality": place_ends((jax.random.randint(key_list[4], (ROWS, NB), 0, 2) < 1).astype(jnp.int32), jax.random.fold_in(key_list[4], 1), 0, 1),
        "grad_out": bell_draw(key_list[5], (ROWS, SEQ_LEN, D), 1.0, 6.0, ((0, 16), (1, 16))),
    }


NEG = -1.0e30


def block_runs(mod_row):
    previous = jnp.concatenate([jnp.zeros((1,), jnp.int32), mod_row[:-1]])
    starts = ((mod_row == 0) | (previous == 0)).astype(jnp.int32)
    return jnp.cumsum(starts).astype(jnp.int32)


def visible(row_start, row_count, mod_tok, run_tok):
    total_len = mod_tok.shape[0]
    query_pos = row_start + jnp.arange(row_count, dtype=jnp.int32)
    key_pos = jnp.arange(total_len, dtype=jnp.int32)
    query_blk = (query_pos // BLOCK)[:, None]
    key_blk = (key_pos // BLOCK)[None, :]
    query_mod = lax.dynamic_slice_in_dim(mod_tok, row_start, row_count)[:, None]
    query_run = lax.dynamic_slice_in_dim(run_tok, row_start, row_count)[:, None]
    same_blk = key_blk == query_blk
    causal = key_pos[None, :] <= query_pos[:, None]
    earlier = key_blk < query_blk
    inside = same_blk & ((query_mod == 1) | causal)
    later = (key_blk > query_blk) & (query_mod == 1) & (run_tok[None, :] == query_run)
    return earlier | inside | later


def probabilities(query_blk, head_k, allowed):
    scale = query_blk.shape[-1] ** -0.5
    scores = lax.dot_general(query_blk, head_k, (((1,), (1,)), ((), ())), preferred_element_type=jnp.float32) * scale
    scores = jnp.where(allowed, scores, NEG)
    row_top = jnp.max(scores, axis=1, keepdims=True)
    weights = jnp.exp(scores - row_top)
    return weights / jnp.sum(weights, axis=1, keepdims=True)


def head_forward(head_q, head_k, head_v, mod_tok, run_tok, query_rows):
    total_len = head_q.shape[0]
    num_blocks = total_len // query_rows

    def query_block(block_idx):
        row_start = (block_idx * query_rows).astype(jnp.int32)
        query_blk = lax.dynamic_slice_in_dim(head_q, row_start, query_rows)
        prob_full = probabilities(query_blk, head_k, visible(row_start, query_rows, mod_tok, run_tok))
        return jnp.dot(prob_full.astype(jnp.bfloat16), head_v, preferred_element_type=jnp.float32).astype(jnp.bfloat16)

    return lax.map(query_block, jnp.arange(num_blocks, dtype=jnp.int32)).reshape(total_len, -1)


def head_backward(head_q, head_k, head_v, head_o, head_do, mod_tok, run_tok, query_rows):
    total_len, head_width = head_q.shape
    num_blocks = total_len // query_rows
    scale = head_width ** -0.5

    def query_block(state_pair, block_idx):
        grad_k, grad_v = state_pair
        row_start = (block_idx * query_rows).astype(jnp.int32)
        query_blk = lax.dynamic_slice_in_dim(head_q, row_start, query_rows)
        out_blk = lax.dynamic_slice_in_dim(head_o, row_start, query_rows)
        dout_blk = lax.dynamic_slice_in_dim(head_do, row_start, query_rows)
        prob_full = probabilities(query_blk, head_k, visible(row_start, query_rows, mod_tok, run_tok))
        prob_low = prob_full.astype(jnp.bfloat16)
        grad_v = grad_v + lax.dot_general(prob_low, dout_blk, (((0,), (0,)), ((), ())), preferred_element_type=jnp.float32)
        grad_prob = lax.dot_general(dout_blk, head_v, (((1,), (1,)), ((), ())), preferred_element_type=jnp.float32)
        row_delta = jnp.sum(dout_blk.astype(jnp.float32) * out_blk.astype(jnp.float32), axis=1, keepdims=True)
        dscore = (prob_full * (grad_prob - row_delta) * scale).astype(jnp.bfloat16)
        grad_q = jnp.dot(dscore, head_k, preferred_element_type=jnp.float32).astype(jnp.bfloat16)
        grad_k = grad_k + lax.dot_general(dscore, query_blk, (((0,), (0,)), ((), ())), preferred_element_type=jnp.float32)
        return (grad_k, grad_v), grad_q

    zero_acc = jnp.zeros((total_len, head_width), jnp.float32)
    (grad_k, grad_v), grad_q = lax.scan(query_block, (zero_acc, zero_acc), jnp.arange(num_blocks, dtype=jnp.int32))
    return grad_q.reshape(total_len, head_width), grad_k.astype(jnp.bfloat16), grad_v.astype(jnp.bfloat16)


def split_heads(block_rows, head_width):
    return block_rows.reshape(block_rows.shape[0], -1, head_width).transpose(1, 0, 2)


def join_heads(stacked):
    return stacked.transpose(1, 0, 2).reshape(stacked.shape[1], -1)


def reference(queries, keys, values, w_out, modality, grad_out):
    query_rows = min(512, SEQ_LEN)
    col_group = D // N_SEQ

    def one_row(grad_total, row_inputs):
        query_row, key_row, value_row, mod_row, grad_row = row_inputs
        run_ids = block_runs(mod_row)
        mod_tok = jnp.repeat(mod_row, BLOCK)
        run_tok = jnp.repeat(run_ids, BLOCK)
        query_heads = split_heads(query_row, HD)
        key_heads = split_heads(key_row, HD)
        value_heads = split_heads(value_row, HD)

        def forward_head(head_inputs):
            return head_forward(head_inputs[0], head_inputs[1], head_inputs[2], mod_tok, run_tok, query_rows)

        out_heads = lax.map(forward_head, (query_heads, key_heads, value_heads))
        attended = join_heads(out_heads)
        out_blocks = attended.reshape(NB, BLOCK, HW)
        grad_blocks = grad_row.reshape(NB, BLOCK, D)

        def project(block_idx):
            weight_sel = lax.dynamic_index_in_dim(w_out, mod_row[block_idx], 0, keepdims=False)
            return jnp.dot(out_blocks[block_idx], weight_sel, preferred_element_type=jnp.float32)

        mixed_row = lax.map(project, jnp.arange(NB, dtype=jnp.int32)).reshape(SEQ_LEN, D).astype(jnp.bfloat16)

        def group_term(grad_sum, group_idx):
            col_start = (group_idx * col_group).astype(jnp.int32)

            def per_block(block_idx):
                weight_sel = lax.dynamic_index_in_dim(w_out, mod_row[block_idx], 0, keepdims=False)
                weight_cols = lax.dynamic_slice_in_dim(weight_sel, col_start, col_group, 1)
                grad_cols = lax.dynamic_slice_in_dim(grad_blocks[block_idx], col_start, col_group, 1)
                return lax.dot_general(grad_cols, weight_cols, (((1,), (1,)), ((), ())), preferred_element_type=jnp.float32)

            group_part = lax.map(per_block, jnp.arange(NB, dtype=jnp.int32)).reshape(SEQ_LEN, HW)
            part_low = lax.optimization_barrier(group_part.astype(jnp.bfloat16))
            return grad_sum + part_low.astype(jnp.float32), None

        grad_sum, unused = lax.scan(group_term, jnp.zeros((SEQ_LEN, HW), jnp.float32), jnp.arange(N_SEQ, dtype=jnp.int32))
        grad_attended = grad_sum.astype(jnp.bfloat16)

        def add_block(block_idx, totals):
            block_term = lax.dot_general(out_blocks[block_idx], grad_blocks[block_idx], (((0,), (0,)), ((), ())), preferred_element_type=jnp.float32)
            current = lax.dynamic_index_in_dim(totals, mod_row[block_idx], 0, keepdims=False)
            return lax.dynamic_update_index_in_dim(totals, current + block_term, mod_row[block_idx], 0)

        row_grad = lax.fori_loop(0, NB, add_block, jnp.zeros((2, HW, D), jnp.float32))
        row_low = lax.optimization_barrier(row_grad.astype(jnp.bfloat16))
        grad_total = grad_total + row_low.astype(jnp.float32)

        def backward_head(head_inputs):
            return head_backward(head_inputs[0], head_inputs[1], head_inputs[2], head_inputs[3], head_inputs[4], mod_tok, run_tok, query_rows)

        grad_q, grad_k, grad_v = lax.map(backward_head, (query_heads, key_heads, value_heads, out_heads, split_heads(grad_attended, HD)))
        return grad_total, (mixed_row, join_heads(grad_q), join_heads(grad_k), join_heads(grad_v))

    grad_total, row_outputs = lax.scan(one_row, jnp.zeros((2, HW, D), jnp.float32), (queries, keys, values, modality, grad_out))
    mixed, grad_queries, grad_keys, grad_values = row_outputs
    return mixed, grad_queries, grad_keys, grad_values, grad_total
```

```python
import functools
import math

import jax
import jax.numpy as jnp
from jax import lax
from jax.experimental import pallas as pl
from jax.experimental.pallas import tpu as pltpu
from jax.sharding import PartitionSpec as P

HD = 128
BLOCK = 128
NX, NY, NZ = 4, 4, 8
NS = 2 * NZ
HALF = NY // 2
NEG = -1e30
MESH = pl.DeviceIdType.MESH
BF = jnp.bfloat16
F32 = jnp.float32


def place():
    dp = lax.axis_index("dp")
    s = lax.axis_index("seq")
    return lax.div(dp, NY), lax.rem(dp, NY), lax.div(s, 2), lax.rem(s, 2), s


def device(x, y, s):
    return {"dp": x * NY + y, "seq": s}


def lanes(start, size):
    return pl.ds(pl.multiple_of(start, 128), size)


def rows(start, size):
    return pl.ds(pl.multiple_of(start, 128), size)


def remote(src, dst, send, recv, where):
    return pltpu.make_async_remote_copy(
        src_ref=src, dst_ref=dst, send_sem=send, recv_sem=recv, device_id=where, device_id_type=MESH
    )


def enter(x, y, z, c, s):
    barrier = pltpu.get_barrier_semaphore()
    count = 0
    others = [device(x, y, lax.rem(s + p, NS)) for p in range(1, NS)]
    for a in range(NX):
        for b in range(NY):
            if a or b:
                others.append(device(lax.rem(x + a, NX), lax.rem(y + b, NY), s))
    for b in range(1, NY):
        others.append(device(x, lax.rem(y + b, NY), 2 * z + 1 - c))
    for other in others:
        pl.semaphore_signal(barrier, inc=1, device_id=other, device_id_type=MESH)
        count += 1
    pl.semaphore_wait(barrier, count)


def gather_kernel(
    mod, q, k, v, w, go,
    qh, kh, vh, gah, wg, gog, masks,
    wbuf, gobuf, gom, part, rsbuf, gasum, mbuf,
    loc, qs, qr, ws, wr, xs, xr, cs, cr, gs, gr, ms, mr, ys, yr, hs, hr, os, orr,
):
    x, y, z, c, s = place()
    dp = x * NY + y
    fs = q.shape[1] // NX
    fc = fs // 2
    enter(x, y, z, c, s)
    sib = device(x, y, 2 * z + 1 - c)
    left = device(lax.rem(x + NX - 1, NX), y, s)
    right = device(lax.rem(x + 1, NX), y, s)
    xl, xr_, xo = lax.rem(x + NX - 1, NX), lax.rem(x + 1, NX), lax.rem(x + 2, NX)

    def wslice(at_x, at_c):
        return wbuf.at[:, rows(at_x * fs + at_c * fc, fc), :]

    def whalf(at_x, at_c, m):
        return wbuf.at[m, rows(at_x * fs + at_c * fc, fc), :]

    holder = c == lax.div(y, HALF)
    wcols = lanes(lax.rem(y, HALF) * 128, 128)

    def w_send(p):
        to = lax.rem(s + p, NS)
        to_c = lax.rem(to, 2)
        spot = rows(x * fs + to_c * fc, fc)
        return remote(
            w.at[:, spot, wcols], wbuf.at[:, spot, lanes(z * 128, 128)],
            ws.at[p - 1], wr.at[z], device(x, y, to),
        )

    own_spot = rows(x * fs + c * fc, fc)
    w_own = pltpu.make_async_copy(
        w.at[:, own_spot, wcols], wbuf.at[:, own_spot, lanes(z * 128, 128)], loc.at[0]
    )

    @pl.when(holder)
    def _():
        w_own.start()
        for p in range(1, NS):
            w_send(p).start()

    mbuf[dp] = jnp.full(mbuf.shape[1:], mod[0, s], jnp.int32).astype(F32).astype(BF)
    mask_copies = []
    for a in range(NX):
        for b in range(NY):
            if a or b:
                i = a * NY + b
                cp = remote(
                    mbuf.at[dp], mbuf.at[dp], ms.at[i], mr.at[i],
                    device(lax.rem(x + a, NX), lax.rem(y + b, NY), s),
                )
                cp.start()
                mask_copies.append(cp)
    go_own = pltpu.make_async_copy(go.at[y], gobuf.at[y], loc.at[1])
    go_own.start()
    go_copies = []
    for d in range(1, NY):
        to = lax.rem(y + d, NY)
        cp = remote(go.at[to], gobuf.at[y], gs.at[d], gr.at[d], device(x, to, s))
        cp.start()
        go_copies.append(cp)

    for i in range(NZ):
        @pl.when(jnp.logical_not(jnp.logical_and(holder, z == i)))
        def _():
            remote(
                wbuf.at[:, own_spot, lanes(i * 128, 128)], wbuf.at[:, own_spot, lanes(i * 128, 128)],
                ws.at[0], wr.at[i], sib,
            ).wait_recv()

    @pl.when(holder)
    def _():
        w_own.wait()

    mine = wslice(x, c)
    to_right = remote(mine, mine, xs.at[0], xr.at[0], right)
    to_left = remote(mine, mine, xs.at[1], xr.at[1], left)
    to_right.start()
    to_left.start()
    to_sib = [remote(mine, mine, cs.at[0], cr.at[0], sib)]
    to_sib[0].start()

    token_spot = rows(s * BLOCK, BLOCK)
    qkv_copies = []
    for i, (src, dst) in enumerate(((q, qh), (k, kh), (v, vh))):
        cp = pltpu.make_async_copy(src.at[:, lanes(s * HD, HD)], dst.at[token_spot], loc.at[2 + i])
        cp.start()
        qkv_copies.append(cp)
    for p in range(1, NS):
        to = lax.rem(s + p, NS)
        for i, (src, dst) in enumerate(((q, qh), (k, kh), (v, vh))):
            cp = remote(
                src.at[:, lanes(to * HD, HD)], dst.at[token_spot],
                qs.at[i, p], qr.at[i, p], device(x, y, to),
            )
            cp.start()
            qkv_copies.append(cp)

    go_own.wait()
    for cp in go_copies:
        cp.wait()
    gog_own = pltpu.make_async_copy(gobuf, gog.at[x], loc.at[5])
    gog_own.start()
    for cp in mask_copies:
        cp.wait()
    for b in range(NY):
        one = mbuf[x * NY + b, 0:1, :]
        zero = (1.0 - one.astype(F32)).astype(BF)
        for j in range(NZ):
            piece = gobuf[b, :, j * 128 : (j + 1) * 128]
            gom[0, b * BLOCK : (b + 1) * BLOCK, j * 128 : (j + 1) * 128] = piece * zero
            gom[1, b * BLOCK : (b + 1) * BLOCK, j * 128 : (j + 1) * 128] = piece * one
    masks[...] = mbuf[...]

    y_copies = {}

    def compute(step, at_x, at_c):
        f = at_x * 2 + at_c
        spot = rows(at_x * fs + at_c * fc, fc)
        cols = lanes(f * fc, fc)
        acc = lax.dot_general(
            gom[0], wbuf[0, spot, :], (((1,), (1,)), ((), ())), preferred_element_type=F32
        ) + lax.dot_general(
            gom[1], wbuf[1, spot, :], (((1,), (1,)), ((), ())), preferred_element_type=F32
        )
        low = acc.astype(BF)
        for b in range(NY):
            part[b, :, cols] = low[b * BLOCK : (b + 1) * BLOCK]
        y_copies[step] = []
        for d in range(1, NY):
            to = lax.rem(y + d, NY)
            cp = remote(
                part.at[to, :, cols], rsbuf.at[y, :, cols], ys.at[step, d], yr.at[step, d],
                device(x, to, s),
            )
            cp.start()
            y_copies[step].append(cp)

    def head_copies(at_x, at_c, h):
        f = at_x * 2 + at_c
        heads = fc // HD
        head = f * heads + h
        src = gasum.at[:, lanes(head * HD, HD)]
        far = remote(src, gah.at[token_spot], hs.at[head], hr.at[s], device(x, y, head))
        near = pltpu.make_async_copy(src, gah.at[token_spot], loc.at[6])
        return head, far, near

    def total(step, at_x, at_c):
        f = at_x * 2 + at_c
        cols = lanes(f * fc, fc)
        for cp in y_copies[step]:
            cp.wait()
        acc = part[y, :, cols].astype(F32)
        for d in range(1, NY):
            acc = acc + rsbuf[lax.rem(y + d, NY), :, cols].astype(F32)
        gasum[:, cols] = acc.astype(BF)
        for h in range(fc // HD):
            head, far, near = head_copies(at_x, at_c, h)

            @pl.when(head == s)
            def _():
                near.start()

            @pl.when(head != s)
            def _():
                far.start()

    order = [(x, c), (x, 1 - c), (xl, c), (xl, 1 - c), (xr_, c), (xr_, 1 - c), (xo, c), (xo, 1 - c)]
    compute(0, *order[0])
    other = wslice(x, 1 - c)
    remote(other, other, cs.at[0], cr.at[0], sib).wait_recv()
    compute(1, *order[1])

    from_left = wslice(xl, c)
    remote(from_left, from_left, xs.at[0], xr.at[0], right).wait_recv()
    on_right = remote(whalf(xl, c, 0), whalf(xl, c, 0), xs.at[2], xr.at[2], right)
    on_right.start()
    cp = remote(from_left, from_left, cs.at[1], cr.at[1], sib)
    cp.start()
    to_sib.append(cp)
    from_right = wslice(xr_, c)
    remote(from_right, from_right, xs.at[1], xr.at[1], left).wait_recv()
    on_left = remote(whalf(xr_, c, 1), whalf(xr_, c, 1), xs.at[3], xr.at[3], left)
    on_left.start()
    cp = remote(from_right, from_right, cs.at[2], cr.at[2], sib)
    cp.start()
    to_sib.append(cp)

    total(0, *order[0])
    total(1, *order[1])
    compute(2, *order[2])
    compute(4, *order[4])
    other = wslice(xl, 1 - c)
    remote(other, other, cs.at[1], cr.at[1], sib).wait_recv()
    compute(3, *order[3])
    other = wslice(xr_, 1 - c)
    remote(other, other, cs.at[2], cr.at[2], sib).wait_recv()
    compute(5, *order[5])
    for step in (2, 4, 3, 5):
        total(step, *order[step])

    opposite = whalf(xo, c, 0)
    remote(opposite, opposite, xs.at[2], xr.at[2], right).wait_recv()
    opposite = whalf(xo, c, 1)
    remote(opposite, opposite, xs.at[3], xr.at[3], left).wait_recv()
    opposite = wslice(xo, c)
    cp = remote(opposite, opposite, cs.at[3], cr.at[3], sib)
    cp.start()
    to_sib.append(cp)

    gog_own.wait()
    go_right = remote(gobuf, gog.at[x], os.at[0], orr.at[0], right)
    go_left = remote(gobuf, gog.at[x], os.at[1], orr.at[1], left)
    go_right.start()
    go_left.start()

    compute(6, *order[6])
    other = wslice(xo, 1 - c)
    remote(other, other, cs.at[3], cr.at[3], sib).wait_recv()
    compute(7, *order[7])
    keep = pltpu.make_async_copy(wbuf, wg, loc.at[7])
    keep.start()
    total(6, *order[6])
    total(7, *order[7])

    remote(gobuf, gog.at[xl], os.at[0], orr.at[0], right).wait_recv()
    go_on_right = remote(
        gog.at[xl, pl.ds(0, HALF)], gog.at[xl, pl.ds(0, HALF)], os.at[2], orr.at[2], right
    )
    go_on_right.start()
    remote(gobuf, gog.at[xr_], os.at[1], orr.at[1], left).wait_recv()
    go_on_left = remote(
        gog.at[xr_, pl.ds(HALF, HALF)], gog.at[xr_, pl.ds(HALF, HALF)], os.at[3], orr.at[3], left
    )
    go_on_left.start()

    for step in range(8):
        for h in range(fc // HD):
            head, far, near = head_copies(*order[step], h)

            @pl.when(head == s)
            def _():
                near.wait()

            @pl.when(head != s)
            def _():
                far.wait_send()

    for p in range(1, NS):
        src = lax.rem(s + NS - p, NS)
        spot = gah.at[rows(src * BLOCK, BLOCK)]
        remote(spot, spot, hs.at[0], hr.at[src], sib).wait_recv()
    for cp in qkv_copies:
        cp.wait()

    @pl.when(holder)
    def _():
        for p in range(1, NS):
            w_send(p).wait_send()

    for cp in to_sib + [to_right, to_left, on_right, on_left, go_right, go_left]:
        cp.wait_send()
    go_on_right.wait()
    go_on_left.wait()
    keep.wait()


def attend_kernel(mod, q, k, v, ga, att, dq, dk, dv, end, s_buf, dk_acc, dv_acc):
    length = q.shape[0]
    blocks = length // BLOCK
    qb = 2 * BLOCK
    kb = 2 * BLOCK
    scale = HD ** -0.5
    c2 = scale * math.log2(math.e)
    end[blocks - 1] = length
    for b in range(blocks - 2, -1, -1):
        end[b] = jnp.where(mod[0, b + 1] == 1, end[b + 1], (b + 1) * BLOCK)
    dk_acc[...] = jnp.zeros_like(dk_acc)
    dv_acc[...] = jnp.zeros_like(dv_acc)
    nt = (((1,), (1,)), ((), ()))
    tn = (((0,), (0,)), ((), ()))

    def strip(i, carry):
        q_rows = pl.ds(pl.multiple_of(i * qb, qb), qb)
        qi = q[q_rows, :]
        gi = ga[q_rows, :]
        row = lax.broadcasted_iota(jnp.int32, (qb, 1), 0)
        b0 = i * 2
        reach0 = jnp.where(mod[0, b0] == 1, end[b0], 0)
        reach1 = jnp.where(mod[0, b0 + 1] == 1, end[b0 + 1], 0)
        limit = jnp.maximum(jnp.where(row < BLOCK, reach0, reach1), row + (i * qb + 1))
        top = jnp.maximum(jnp.maximum(reach0, reach1), (i + 1) * qb)
        n = lax.div(top + kb - 1, kb)

        def scores(j):
            kj = k[pl.ds(pl.multiple_of(j * kb, kb), kb), :]
            return lax.dot_general(qi, kj, nt, preferred_element_type=F32)

        def fold(m, sc):
            for t in range(kb // 128):
                m = jnp.maximum(m, sc[:, t * 128 : (t + 1) * 128])
            return m

        def open_chunk(j, m):
            sc = scores(j)
            s_buf[j] = sc
            return fold(m, sc)

        def masked_chunk(j, m):
            sc = scores(j)
            col = lax.broadcasted_iota(jnp.int32, (qb, kb), 1) + j * kb
            sc = jnp.where(col < limit, sc, NEG)
            s_buf[j] = sc
            return fold(m, sc)

        m = jnp.full((qb, 128), NEG, F32)
        m = lax.fori_loop(0, i, open_chunk, m)
        m = lax.fori_loop(i, n, masked_chunk, m)
        m = jnp.max(m, axis=1, keepdims=True)

        def weigh(j, total):
            e = jnp.exp2((s_buf[j] - m) * c2)
            s_buf[j] = e
            for t in range(kb // 128):
                total = total + e[:, t * 128 : (t + 1) * 128]
            return total

        total = lax.fori_loop(0, n, weigh, jnp.zeros((qb, 128), F32))
        inv = 1.0 / jnp.sum(total, axis=1, keepdims=True)

        def forward(j, acc):
            k_rows = pl.ds(pl.multiple_of(j * kb, kb), kb)
            p = s_buf[j] * inv
            s_buf[j] = p
            low = p.astype(BF)
            dv_acc[k_rows, :] += lax.dot_general(low, gi, tn, preferred_element_type=F32)
            return acc + jnp.dot(low, v[k_rows, :], preferred_element_type=F32)

        out = lax.fori_loop(0, n, forward, jnp.zeros((qb, HD), F32)).astype(BF)
        att[q_rows, :] = out
        delta = jnp.sum(gi.astype(F32) * out.astype(F32), axis=1, keepdims=True)

        def backward(j, acc):
            k_rows = pl.ds(pl.multiple_of(j * kb, kb), kb)
            dp = lax.dot_general(gi, v[k_rows, :], nt, preferred_element_type=F32)
            ds = (s_buf[j] * ((dp - delta) * scale)).astype(BF)
            dk_acc[k_rows, :] += lax.dot_general(ds, qi, tn, preferred_element_type=F32)
            return acc + jnp.dot(ds, k[k_rows, :], preferred_element_type=F32)

        dq[q_rows, :] = lax.fori_loop(0, n, backward, jnp.zeros((qb, HD), F32)).astype(BF)
        return carry

    lax.fori_loop(0, length // qb, strip, 0)
    dk[...] = dk_acc[...].astype(BF)
    dv[...] = dv_acc[...].astype(BF)


def project_kernel(
    att, dq, dk, dv, wg, gog, masks,
    mixt, dqo, dko, dvo, gwo,
    aall, gatt, wv, gov, am, gm, mixp, gws, gwr, gwp, gwz, zbuf, fin,
    loc, hs, hr, ps, pr, ys, yr, qs, qr, xs, xr, cs, cr, zs, zr, fs_, fr,
):
    x, y, z, c, s = place()
    width = wg.shape[1]
    fs = width // NX
    fc = fs // 2
    cols = wg.shape[2]
    tokens = NX * NY * BLOCK
    enter(x, y, z, c, s)
    sib = device(x, y, 2 * z + 1 - c)

    head_spot = lanes(s * HD, HD)
    a_own = pltpu.make_async_copy(att.at[rows(s * BLOCK, BLOCK)], aall.at[y, :, head_spot], loc.at[0])
    a_own.start()
    a_copies = []
    for p in range(1, NS):
        to = lax.rem(s + p, NS)
        cp = remote(
            att.at[rows(to * BLOCK, BLOCK)], aall.at[y, :, head_spot], hs.at[p], hr.at[p],
            device(x, y, to),
        )
        cp.start()
        a_copies.append(cp)
    load_go = pltpu.make_async_copy(gog, gov, loc.at[1])
    load_w = pltpu.make_async_copy(wg, wv, loc.at[2])
    load_go.start()
    load_w.start()
    a_own.wait()
    for cp in a_copies:
        cp.wait()

    p_copies = []
    for a in range(1, NX):
        to_x = lax.rem(x + a, NX)
        for b in range(NY):
            i = a * NY + b
            cp = remote(
                aall.at[y, :, lanes(to_x * fs, fs)], gatt.at[x * NY + y], ps.at[i], pr.at[i],
                device(to_x, lax.rem(y + b, NY), s),
            )
            cp.start()
            p_copies.append(cp)
    y_copies = []
    for d in range(1, NY):
        cp = remote(aall.at[y], aall.at[y], ys.at[d], yr.at[d], device(x, lax.rem(y + d, NY), s))
        cp.start()
        y_copies.append(cp)
    q_copies = []
    for i, (src, dst) in enumerate(((dq, dqo), (dk, dko), (dv, dvo))):
        cp = pltpu.make_async_copy(src.at[rows(s * BLOCK, BLOCK)], dst.at[:, head_spot], loc.at[3 + i])
        cp.start()
        q_copies.append(cp)
    for p in range(1, NS):
        to = lax.rem(s + p, NS)
        for i, (src, dst) in enumerate(((dq, dqo), (dk, dko), (dv, dvo))):
            cp = remote(
                src.at[rows(to * BLOCK, BLOCK)], dst.at[:, head_spot], qs.at[i, p], qr.at[i, p],
                device(x, y, to),
            )
            cp.start()
            q_copies.append(cp)

    for cp in p_copies:
        cp.wait()
    for cp in y_copies:
        cp.wait()
    for b in range(NY):
        gatt[x * NY + b] = aall[b, :, lanes(x * fs, fs)]

    def spread(t, carry):
        one = masks[t, 0:1, :]
        zero = (1.0 - one.astype(F32)).astype(BF)
        spot = pl.ds(pl.multiple_of(t * BLOCK, BLOCK), BLOCK)
        for j in range(fs // 128):
            piece = gatt[t, :, j * 128 : (j + 1) * 128]
            gm[spot, j * 128 : (j + 1) * 128] = piece * zero
            gm[spot, fs + j * 128 : fs + (j + 1) * 128] = piece * one
        return carry

    lax.fori_loop(0, NX * NY, spread, 0)
    load_go.wait()
    tn = (((0,), (0,)), ((), ()))
    step = 256

    def theirs(t, carry):
        spot = pl.ds(pl.multiple_of(t * step, step), step)
        for m in range(2):
            lhs = gm[:, lanes(m * fs + (1 - c) * fc, fc)]
            gws[m, :, spot] = lax.dot_general(
                lhs, gov[:, spot], tn, preferred_element_type=F32
            ).astype(BF)
        return carry

    lax.fori_loop(0, cols // step, theirs, 0)
    swap = remote(gws, gwr, cs.at[0], cr.at[0], sib)
    swap.start()

    def ours(t, carry):
        spot = pl.ds(pl.multiple_of(t * step, step), step)
        for m in range(2):
            lhs = gm[:, lanes(m * fs + c * fc, fc)]
            gwp[m, :, spot] = lax.dot_general(lhs, gov[:, spot], tn, preferred_element_type=F32)
        return carry

    lax.fori_loop(0, cols // step, ours, 0)
    swap.wait()
    for i in range(NZ):
        spot = slice(i * 128, (i + 1) * 128)
        for m in range(2):
            gwz[i, m] = (gwp[m, :, spot] + gwr[m, :, spot].astype(F32)).astype(BF)
    z_copies = []
    for d in range(1, NZ):
        to = lax.rem(z + d, NZ)
        cp = remote(gwz.at[to], zbuf.at[z], zs.at[d], zr.at[d], device(x, y, 2 * to + c))
        cp.start()
        z_copies.append(cp)

    for b in range(NY):
        one = masks[x * NY + b, 0:1, :]
        zero = (1.0 - one.astype(F32)).astype(BF)
        for j in range(width // 128):
            piece = aall[b, :, j * 128 : (j + 1) * 128]
            am[0, b * BLOCK : (b + 1) * BLOCK, j * 128 : (j + 1) * 128] = piece * zero
            am[1, b * BLOCK : (b + 1) * BLOCK, j * 128 : (j + 1) * 128] = piece * one
    load_w.wait()

    def mix(t, carry):
        spot = pl.ds(pl.multiple_of(t * step, step), step)
        acc = jnp.dot(am[0], wv[0, :, spot], preferred_element_type=F32)
        acc = acc + jnp.dot(am[1], wv[1, :, spot], preferred_element_type=F32)
        low = acc.astype(BF)
        for b in range(NY):
            mixp[b, :, spot] = low[b * BLOCK : (b + 1) * BLOCK]
        return carry

    lax.fori_loop(0, cols // step, mix, 0)
    m_own = pltpu.make_async_copy(mixp.at[y], mixt.at[y], loc.at[6])
    m_own.start()
    m_copies = []
    for d in range(1, NY):
        to = lax.rem(y + d, NY)
        cp = remote(mixp.at[to], mixt.at[y], xs.at[d], xr.at[d], device(x, to, s))
        cp.start()
        m_copies.append(cp)

    for cp in z_copies:
        cp.wait()
    for m in range(2):
        acc = gwz[z, m].astype(F32)
        for d in range(1, NZ):
            acc = acc + zbuf[lax.rem(z + d, NZ), m].astype(F32)
        for j in range(HALF):
            fin[j, m] = acc[j * 128 : (j + 1) * 128]
    spot = lanes(lax.rem(y, HALF) * 128, 128)
    for j in range(HALF):
        to_y = c * HALF + j
        to_c = lax.div(y, HALF)
        here = jnp.logical_and(to_y == y, to_c == c)
        near = pltpu.make_async_copy(fin.at[j], gwo.at[:, :, spot], loc.at[7])
        far = remote(
            fin.at[j], gwo.at[:, :, spot], fs_.at[j], fr.at[lax.rem(y, HALF)],
            device(x, to_y, 2 * z + to_c),
        )

        @pl.when(here)
        def _():
            near.start()
            near.wait()

        @pl.when(jnp.logical_not(here))
        def _():
            far.start()
            far.wait_send()

    for i in range(HALF):
        from_y = c * HALF + i
        from_c = lax.div(y, HALF)
        here = jnp.logical_and(from_y == y, from_c == c)

        @pl.when(jnp.logical_not(here))
        def _():
            place_ = gwo.at[:, :, pl.ds(i * 128, 128)]
            remote(fin.at[0], place_, fs_.at[0], fr.at[i], sib).wait_recv()

    m_own.wait()
    for cp in m_copies + q_copies:
        cp.wait()


def any_spec(n):
    return [pl.BlockSpec(memory_space=pl.ANY)] * n


def local(queries, keys, values, w_out, modality, grad_out):
    dma = pltpu.SemaphoreType.DMA
    tokens = queries.shape[1]
    width = queries.shape[2]
    length = tokens * NS
    group = NZ * 128
    shape = jax.ShapeDtypeStruct
    vmem = pl.BlockSpec(memory_space=pltpu.VMEM)
    smem = pl.BlockSpec(memory_space=pltpu.SMEM)
    go = grad_out[0].reshape(tokens, NZ, NY, 128).transpose(2, 0, 1, 3).reshape(NY, tokens, group)
    head = shape((length, HD), BF)
    qh, kh, vh, gah, wg, gog, masks = pl.pallas_call(
        gather_kernel,
        out_shape=(
            head, head, head, head,
            shape((2, width, group), BF),
            shape((NX, NY, BLOCK, group), BF),
            shape((NX * NY, 16, 128), BF),
        ),
        in_specs=[smem] + any_spec(5),
        out_specs=tuple(any_spec(6) + [vmem]),
        scratch_shapes=[
            pltpu.VMEM((2, width, group), BF),
            pltpu.VMEM((NY, BLOCK, group), BF),
            pltpu.VMEM((2, NY * BLOCK, group), BF),
            pltpu.VMEM((NY, BLOCK, width), BF),
            pltpu.VMEM((NY, BLOCK, width), BF),
            pltpu.VMEM((BLOCK, width), BF),
            pltpu.VMEM((NX * NY, 16, 128), BF),
            dma((8,)),
            dma((3, NS)), dma((3, NS)),
            dma((NS,)), dma((NZ,)),
            dma((4,)), dma((4,)),
            dma((4,)), dma((4,)),
            dma((NY,)), dma((NY,)),
            dma((NX * NY,)), dma((NX * NY,)),
            dma((8, NY)), dma((8, NY)),
            dma((NS,)), dma((NS,)),
            dma((4,)), dma((4,)),
        ],
        compiler_params=pltpu.CompilerParams(
            collective_id=0, has_side_effects=True, vmem_limit_bytes=40 << 20
        ),
        name="gather",
    )(modality, queries[0], keys[0], values[0], w_out, go)

    att, dq, dk, dv = pl.pallas_call(
        attend_kernel,
        out_shape=(head, head, head, head),
        in_specs=[smem] + [vmem] * 4,
        out_specs=(vmem,) * 4,
        scratch_shapes=[
            pltpu.SMEM((length // BLOCK,), jnp.int32),
            pltpu.VMEM((length // 256, 256, 256), F32),
            pltpu.VMEM((length, HD), F32),
            pltpu.VMEM((length, HD), F32),
        ],
        compiler_params=pltpu.CompilerParams(vmem_limit_bytes=40 << 20),
        name="attend",
    )(modality, qh, kh, vh, gah)

    fs = width // NX
    all_tokens = NX * NY * BLOCK
    flat = shape((tokens, width), BF)
    mixt, dqo, dko, dvo, gwo = pl.pallas_call(
        project_kernel,
        out_shape=(
            shape((NY, BLOCK, group), BF), flat, flat, flat,
            shape((2, 128, HALF * 128), F32),
        ),
        in_specs=any_spec(6) + [vmem],
        out_specs=tuple(any_spec(5)),
        scratch_shapes=[
            pltpu.VMEM((NY, BLOCK, width), BF),
            pltpu.VMEM((NX * NY, BLOCK, fs), BF),
            pltpu.VMEM((2, width, group), BF),
            pltpu.VMEM((all_tokens, group), BF),
            pltpu.VMEM((2, NY * BLOCK, width), BF),
            pltpu.VMEM((all_tokens, 2 * fs), BF),
            pltpu.VMEM((NY, BLOCK, group), BF),
            pltpu.VMEM((2, fs // 2, group), BF),
            pltpu.VMEM((2, fs // 2, group), BF),
            pltpu.VMEM((2, fs // 2, group), F32),
            pltpu.VMEM((NZ, 2, fs // 2, 128), BF),
            pltpu.VMEM((NZ, 2, fs // 2, 128), BF),
            pltpu.VMEM((HALF, 2, 128, 128), F32),
            dma((8,)),
            dma((NS,)), dma((NS,)),
            dma((NX * NY,)), dma((NX * NY,)),
            dma((NY,)), dma((NY,)),
            dma((3, NS)), dma((3, NS)),
            dma((NY,)), dma((NY,)),
            dma((1,)), dma((1,)),
            dma((NZ,)), dma((NZ,)),
            dma((HALF,)), dma((HALF,)),
        ],
        compiler_params=pltpu.CompilerParams(
            collective_id=1, has_side_effects=True, vmem_limit_bytes=52 << 20
        ),
        name="project",
    )(att, dq, dk, dv, wg, gog.reshape(all_tokens, group), masks)
    mixed = mixt.reshape(NY, tokens, NZ, 128).transpose(1, 2, 0, 3).reshape(1, tokens, NZ * NY * 128)
    return mixed, dqo[None], dko[None], dvo[None], gwo


def solution(mesh):
    return jax.shard_map(
        local,
        mesh=mesh,
        in_specs=(
            P("dp", "seq", None),
            P("dp", "seq", None),
            P("dp", "seq", None),
            P(None, None, "seq"),
            P("dp", None),
            P("dp", "seq", None),
        ),
        out_specs=(
            P("dp", "seq", None),
            P("dp", "seq", None),
            P("dp", "seq", None),
            P("dp", "seq", None),
            P(None, "dp", "seq"),
        ),
        check_vma=False,
    )
```

```python
import functools
import math

import jax
import jax.numpy as jnp
from jax import lax
from jax.experimental import pallas as pl
from jax.experimental.pallas import tpu as pltpu
from jax.sharding import PartitionSpec as P

HD = 128
BLOCK = 128
NX, NY, NZ = 4, 4, 8
NS = 2 * NZ
HALF = NY // 2
NEG = -1e30
MESH = pl.DeviceIdType.MESH
BF = jnp.bfloat16
F32 = jnp.float32


def place():
    dp = lax.axis_index("dp")
    s = lax.axis_index("seq")
    return lax.div(dp, NY), lax.rem(dp, NY), lax.div(s, 2), lax.rem(s, 2), s


def device(x, y, s):
    return {"dp": x * NY + y, "seq": s}


def lanes(start, size):
    return pl.ds(pl.multiple_of(start, 128), size)


def rows(start, size):
    return pl.ds(pl.multiple_of(start, 128), size)


def remote(src, dst, send, recv, where):
    return pltpu.make_async_remote_copy(
        src_ref=src, dst_ref=dst, send_sem=send, recv_sem=recv, device_id=where, device_id_type=MESH
    )


def enter(x, y, z, c, s, cross):
    barrier = pltpu.get_barrier_semaphore()
    others = [device(x, y, lax.rem(s + p, NS)) for p in range(1, NS)]
    others += [device(lax.rem(x + a, NX), y, s) for a in range(1, NX)]
    others += [device(x, lax.rem(y + b, NY), s) for b in range(1, NY)]
    if cross:
        others += [device(x, lax.rem(y + b, NY), 2 * z + 1 - c) for b in range(1, NY)]
    for other in others:
        pl.semaphore_signal(barrier, inc=1, device_id=other, device_id_type=MESH)
    pl.semaphore_wait(barrier, len(others))


def gather_kernel(
    mod, q, k, v, w, go,
    qh, kh, vh, gah, wg, gog, masks,
    wbuf, gobuf, gom, part, rsbuf, gasum, mbuf,
    loc, qs, qr, ws, wr, xs, xr, cs, cr, gs, gr, ms, mr, ys, yr, hs, hr, os, orr,
):
    x, y, z, c, s = place()
    dp = x * NY + y
    fs = q.shape[1] // NX
    fc = fs // 2
    enter(x, y, z, c, s, False)
    sib = device(x, y, 2 * z + 1 - c)
    left = device(lax.rem(x + NX - 1, NX), y, s)
    right = device(lax.rem(x + 1, NX), y, s)
    xl, xr_, xo = lax.rem(x + NX - 1, NX), lax.rem(x + 1, NX), lax.rem(x + 2, NX)

    def whalf(at_x, at_c, m):
        return wbuf.at[m, rows(at_x * fs + at_c * fc, fc), :]

    holder = c == lax.div(y, HALF)
    wcols = lanes(lax.rem(y, HALF) * 128, 128)

    def w_send(m, p):
        to = lax.rem(s + p, NS)
        to_c = lax.rem(to, 2)
        spot = rows(x * fs + to_c * fc, fc)
        return remote(
            w.at[m, spot, wcols], wbuf.at[m, spot, lanes(z * 128, 128)],
            ws.at[m, p], wr.at[m, z], device(x, y, to),
        )

    own_spot = rows(x * fs + c * fc, fc)
    w_own = pltpu.make_async_copy(
        w.at[:, own_spot, wcols], wbuf.at[:, own_spot, lanes(z * 128, 128)], loc.at[0]
    )

    @pl.when(holder)
    def _():
        w_own.start()
        for m in range(2):
            for p in range(1, NS):
                w_send(m, p).start()

    mbuf[dp] = jnp.full(mbuf.shape[1:], mod[0, s], jnp.int32).astype(F32).astype(BF)
    mask_copies = []
    for d in range(1, NY):
        cp = remote(
            mbuf.at[dp], mbuf.at[dp], ms.at[d], mr.at[d], device(x, lax.rem(y + d, NY), s)
        )
        cp.start()
        mask_copies.append(cp)
    for i in range(NZ):
        pltpu.make_async_copy(
            go.at[:, lanes((i * NY + y) * 128, 128)], gobuf.at[y, :, pl.ds(i * 128, 128)], loc.at[1]
        ).start()
    go_own = pltpu.make_async_copy(gobuf.at[y], gobuf.at[y], loc.at[1])
    go_copies = []
    for d in range(1, NY):
        to = lax.rem(y + d, NY)
        for i in range(NZ):
            remote(
                go.at[:, lanes((i * NY + to) * 128, 128)], gobuf.at[y, :, pl.ds(i * 128, 128)],
                gs.at[d], gr.at[d], device(x, to, s),
            ).start()
        src = lax.rem(y + NY - d, NY)
        go_copies.append(remote(gobuf.at[y], gobuf.at[src], gs.at[d], gr.at[d], device(x, to, s)))

    @pl.when(holder)
    def _():
        w_own.wait()

    sent = []
    for m in range(2):
        for i in range(NZ):
            spot = wbuf.at[m, own_spot, pl.ds(i * 128, 128)]

            @pl.when(jnp.logical_not(jnp.logical_and(holder, z == i)))
            def _():
                remote(spot, spot, ws.at[m, 0], wr.at[m, i], sib).wait_recv()

        mine = whalf(x, c, m)
        for cp in (
            remote(mine, mine, xs.at[0, m], xr.at[0, m], right),
            remote(mine, mine, xs.at[1, m], xr.at[1, m], left),
            remote(mine, mine, cs.at[0, m], cr.at[0, m], sib),
        ):
            cp.start()
            sent.append(cp)

    token_spot = rows(s * BLOCK, BLOCK)
    qkv_copies = []
    for i, (src, dst) in enumerate(((q, qh), (k, kh), (v, vh))):
        cp = pltpu.make_async_copy(src.at[:, lanes(s * HD, HD)], dst.at[token_spot], loc.at[2 + i])
        cp.start()
        qkv_copies.append(cp)
    for p in range(1, NS):
        to = lax.rem(s + p, NS)
        for i, (src, dst) in enumerate(((q, qh), (k, kh), (v, vh))):
            cp = remote(
                src.at[:, lanes(to * HD, HD)], dst.at[token_spot],
                qs.at[i, p], qr.at[i, p], device(x, y, to),
            )
            cp.start()
            qkv_copies.append(cp)

    go_own.wait()
    for cp in go_copies:
        cp.wait()
    gog_own = pltpu.make_async_copy(gobuf, gog.at[x], loc.at[5])
    gog_own.start()
    for d in range(1, NY):
        spot = mbuf.at[x * NY + lax.rem(y + NY - d, NY)]
        mask_copies[d - 1].wait_send()
        remote(spot, spot, ms.at[d], mr.at[d], sib).wait_recv()
    mask_copies = []
    for a in range(1, NX):
        spot = mbuf.at[pl.ds(x * NY, NY)]
        cp = remote(spot, spot, ms.at[NY + a], mr.at[NY + a], device(lax.rem(x + a, NX), y, s))
        cp.start()
        mask_copies.append(cp)
    for b in range(NY):
        one = mbuf[x * NY + b, 0:1, :]
        zero = (1.0 - one.astype(F32)).astype(BF)
        for j in range(NZ):
            piece = gobuf[b, :, j * 128 : (j + 1) * 128]
            gom[0, b * BLOCK : (b + 1) * BLOCK, j * 128 : (j + 1) * 128] = piece * zero
            gom[1, b * BLOCK : (b + 1) * BLOCK, j * 128 : (j + 1) * 128] = piece * one
    y_copies = {}

    def compute(step, at_x, at_c):
        f = at_x * 2 + at_c
        spot = rows(at_x * fs + at_c * fc, fc)
        cols = lanes(f * fc, fc)
        acc = lax.dot_general(
            gom[0], wbuf[0, spot, :], (((1,), (1,)), ((), ())), preferred_element_type=F32
        ) + lax.dot_general(
            gom[1], wbuf[1, spot, :], (((1,), (1,)), ((), ())), preferred_element_type=F32
        )
        low = acc.astype(BF)
        for b in range(NY):
            part[b, :, cols] = low[b * BLOCK : (b + 1) * BLOCK]
        y_copies[step] = []
        for d in range(1, NY):
            to = lax.rem(y + d, NY)
            cp = remote(
                part.at[to, :, cols], rsbuf.at[y, :, cols], ys.at[step, d], yr.at[step, d],
                device(x, to, s),
            )
            cp.start()
            y_copies[step].append(cp)

    def head_copies(at_x, at_c, h):
        f = at_x * 2 + at_c
        heads = fc // HD
        head = f * heads + h
        src = gasum.at[:, lanes(head * HD, HD)]
        far = remote(src, gah.at[token_spot], hs.at[head], hr.at[s], device(x, y, head))
        near = pltpu.make_async_copy(src, gah.at[token_spot], loc.at[6])
        return head, far, near

    def total(step, at_x, at_c):
        f = at_x * 2 + at_c
        cols = lanes(f * fc, fc)
        for cp in y_copies[step]:
            cp.wait()
        acc = part[y, :, cols].astype(F32)
        for d in range(1, NY):
            acc = acc + rsbuf[lax.rem(y + d, NY), :, cols].astype(F32)
        gasum[:, cols] = acc.astype(BF)
        for h in range(fc // HD):
            head, far, near = head_copies(at_x, at_c, h)

            @pl.when(head == s)
            def _():
                near.start()

            @pl.when(head != s)
            def _():
                far.start()

    def arrive(side, at_x, m):
        spot = whalf(at_x, c, m)
        remote(spot, spot, xs.at[side, m], xr.at[side, m], sib).wait_recv()
        cp = remote(spot, spot, cs.at[side + 1, m], cr.at[side + 1, m], sib)
        cp.start()
        sent.append(cp)

    def onward(at_x, m, where):
        spot = whalf(at_x, c, m)
        cp = remote(spot, spot, xs.at[2, m], xr.at[2, m], where)
        cp.start()
        sent.append(cp)

    def other_core(i, at_x):
        for m in range(2):
            spot = whalf(at_x, 1 - c, m)
            remote(spot, spot, cs.at[i, m], cr.at[i, m], sib).wait_recv()

    order = [(x, c), (x, 1 - c), (xl, c), (xl, 1 - c), (xr_, c), (xr_, 1 - c), (xo, c), (xo, 1 - c)]
    compute(0, *order[0])
    arrive(0, xl, 0)
    onward(xl, 0, right)
    arrive(1, xr_, 0)
    other_core(0, x)
    compute(1, *order[1])
    total(0, *order[0])
    arrive(1, xr_, 1)
    onward(xr_, 1, left)
    arrive(0, xl, 1)
    total(1, *order[1])
    compute(2, *order[2])
    compute(4, *order[4])
    other_core(1, xl)
    compute(3, *order[3])
    other_core(2, xr_)
    compute(5, *order[5])
    total(2, *order[2])
    total(4, *order[4])
    arrive(2, xo, 0)
    total(3, *order[3])
    total(5, *order[5])
    arrive(2, xo, 1)

    gog_own.wait()
    go_right = remote(gobuf, gog.at[x], os.at[0], orr.at[0], right)
    go_left = remote(gobuf, gog.at[x], os.at[1], orr.at[1], left)
    go_right.start()
    go_left.start()

    compute(6, *order[6])
    other_core(3, xo)
    compute(7, *order[7])
    keep = pltpu.make_async_copy(wbuf, wg, loc.at[7])
    keep.start()
    total(6, *order[6])
    total(7, *order[7])

    for step in range(8):
        for h in range(fc // HD):
            head, far, near = head_copies(*order[step], h)

            @pl.when(head == s)
            def _():
                near.wait()

            @pl.when(head != s)
            def _():
                far.wait_send()

    for p in range(1, NS):
        src = lax.rem(s + NS - p, NS)
        spot = gah.at[rows(src * BLOCK, BLOCK)]
        remote(spot, spot, hs.at[0], hr.at[src], sib).wait_recv()
    for cp in qkv_copies:
        cp.wait()

    @pl.when(holder)
    def _():
        for m in range(2):
            for p in range(1, NS):
                w_send(m, p).wait_send()

    for cp in sent:
        cp.wait_send()
    for a in range(1, NX):
        spot = mbuf.at[pl.ds(lax.rem(x + NX - a, NX) * NY, NY)]
        mask_copies[a - 1].wait_send()
        remote(spot, spot, ms.at[NY + a], mr.at[NY + a], sib).wait_recv()
    masks[...] = mbuf[...]
    go_right.wait()
    go_left.wait()
    keep.wait()


def attend_kernel(mod, q, k, v, ga, att, dq, dk, dv, end, s_buf, dk_t, dv_t):
    length = q.shape[0]
    blocks = length // BLOCK
    qb = 2 * BLOCK
    kb = 2 * BLOCK
    strips = length // qb
    scale = HD ** -0.5
    c2 = scale * math.log2(math.e)
    end[blocks - 1] = length
    for b in range(blocks - 2, -1, -1):
        end[b] = jnp.where(mod[0, b + 1] == 1, end[b + 1], (b + 1) * BLOCK)
    dk_t[...] = jnp.zeros_like(dk_t)
    dv_t[...] = jnp.zeros_like(dv_t)
    nt = (((1,), (1,)), ((), ()))
    row = lax.broadcasted_iota(jnp.int32, (qb, 1), 0)

    for i in range(strips):
        q_rows = pl.ds(i * qb, qb)
        buf = s_buf.at[i % 2]
        qi = q[q_rows, :]
        gi = ga[q_rows, :].astype(F32)
        reach0 = jnp.where(mod[0, 2 * i] == 1, end[2 * i], 0)
        reach1 = jnp.where(mod[0, 2 * i + 1] == 1, end[2 * i + 1], 0)
        limit = jnp.maximum(jnp.where(row < BLOCK, reach0, reach1), row + (i * qb + 1))
        n = lax.div(jnp.maximum(jnp.maximum(reach0, reach1), (i + 1) * qb) + (kb - 1), kb)

        def part(j):
            return pl.ds(j * kb if isinstance(j, int) else pl.multiple_of(j * kb, kb), kb)

        def chunks(body, carry):
            for j in range(i + 1):
                carry = body(j, carry)
            if i + 1 < strips:
                carry = lax.fori_loop(i + 1, n, body, carry)
            return carry

        def scores(j, m):
            sc = lax.dot_general(qi, k[part(j), :], nt, preferred_element_type=F32)
            if not isinstance(j, int) or j == i:
                col = lax.broadcasted_iota(jnp.int32, (qb, kb), 1) + j * kb
                sc = jnp.where(col < limit, sc, NEG)
            buf[j] = sc
            for t in range(kb // 128):
                m = jnp.maximum(m, sc[:, t * 128 : (t + 1) * 128])
            return m

        m = chunks(scores, jnp.full((qb, 128), NEG, F32))
        m = jnp.max(m, axis=1, keepdims=True)

        def forward(j, carry):
            total, acc = carry
            e = jnp.exp2((buf[j] - m) * c2)
            buf[j] = e
            for t in range(kb // 128):
                total = total + e[:, t * 128 : (t + 1) * 128]
            return total, acc + jnp.dot(e.astype(BF), v[part(j), :], preferred_element_type=F32)

        total, acc = chunks(forward, (jnp.zeros((qb, 128), F32), jnp.zeros((qb, HD), F32)))
        inv = 1.0 / jnp.sum(total, axis=1, keepdims=True)
        out = (acc * inv).astype(BF)
        att[q_rows, :] = out
        gl = gi * inv
        delta = jnp.sum(gl * out.astype(F32), axis=1, keepdims=True)
        gl = gl.astype(BF)
        gt = gl.T
        qt = qi.T

        def backward(j, acc):
            e = buf[j]
            dp = lax.dot_general(gl, v[part(j), :], nt, preferred_element_type=F32)
            ds = (e * (dp - delta)).astype(BF)
            dv_t[:, part(j)] += jnp.dot(gt, e.astype(BF), preferred_element_type=F32)
            dk_t[:, part(j)] += jnp.dot(qt, ds, preferred_element_type=F32)
            return acc + jnp.dot(ds, k[part(j), :], preferred_element_type=F32)

        acc = chunks(backward, jnp.zeros((qb, HD), F32))
        dq[q_rows, :] = (acc * scale).astype(BF)

    for i in range(strips):
        spot = slice(i * qb, (i + 1) * qb)
        dk[spot, :] = (dk_t[:, spot].T * scale).astype(BF)
        dv[spot, :] = dv_t[:, spot].T.astype(BF)


def project_kernel(
    att, dq, dk, dv, wg, gog, masks,
    mixo, dqo, dko, dvo, gwo,
    aall, gatt, wv, gov, am, gm, mixp, gws, gwr, gwz, zbuf, fin,
    loc, hs, hr, ps, pr, ys, yr, qs, qr, xs, xr, cs, cr, zs, zr, fs_, fr, os, orr,
):
    x, y, z, c, s = place()
    width = wg.shape[1]
    fs = width // NX
    fc = fs // 2
    cols = wg.shape[2]
    tokens = NX * NY * BLOCK
    enter(x, y, z, c, s, True)
    sib = device(x, y, 2 * z + 1 - c)

    head_spot = lanes(s * HD, HD)
    a_own = pltpu.make_async_copy(att.at[rows(s * BLOCK, BLOCK)], aall.at[y, :, head_spot], loc.at[0])
    a_own.start()
    a_copies = []
    for p in range(1, NS):
        to = lax.rem(s + p, NS)
        cp = remote(
            att.at[rows(to * BLOCK, BLOCK)], aall.at[y, :, head_spot], hs.at[p], hr.at[p],
            device(x, y, to),
        )
        cp.start()
        a_copies.append(cp)
    xl, xo, xr_ = lax.rem(x + NX - 1, NX), lax.rem(x + 2, NX), lax.rem(x + 1, NX)
    left, right = device(xl, y, s), device(xr_, y, s)
    half = HALF * BLOCK

    def go_part(at_x, h):
        return pl.ds(pl.multiple_of(at_x * (NY * BLOCK) + h * half, half), half)

    on_right = remote(gog.at[go_part(xl, 0)], gov.at[go_part(xl, 0)], os.at[0], orr.at[0], right)
    on_left = remote(gog.at[go_part(xr_, 1)], gov.at[go_part(xr_, 1)], os.at[1], orr.at[1], left)
    on_right.start()
    on_left.start()
    load_go = []
    for i, at_x in enumerate((x, xl, xr_)):
        spot = pl.ds(pl.multiple_of(at_x * (NY * BLOCK), NY * BLOCK), NY * BLOCK)
        cp = pltpu.make_async_copy(gog.at[spot], gov.at[spot], loc.at[8 + i])
        cp.start()
        load_go.append(cp)
    load_w = pltpu.make_async_copy(wg, wv, loc.at[2])
    load_w.start()
    a_own.wait()
    for cp in a_copies:
        cp.wait()

    def y_copy(block, d, a):
        spot = aall.at[block, :, lanes(lax.rem(x + a, NX) * fs, fs)]
        return remote(spot, spot, ys.at[d, a], yr.at[d, a], device(x, lax.rem(y + d, NY), s))

    def x_copy(block, d, a):
        to_x = lax.rem(x + a, NX)
        return remote(
            aall.at[block, :, lanes(to_x * fs, fs)], gatt.at[x * NY + block],
            ps.at[d, a], pr.at[d, a], device(to_x, y, s),
        )

    for a in (1, 3, 2):
        for d in (1, 3, 2):
            y_copy(y, d, a).start()
        x_copy(y, 0, a).start()
    for d in (1, 3, 2):
        y_copy(y, d, 0).start()
    q_copies = []
    for i, (src, dst) in enumerate(((dq, dqo), (dk, dko), (dv, dvo))):
        cp = pltpu.make_async_copy(src.at[rows(s * BLOCK, BLOCK)], dst.at[:, head_spot], loc.at[3 + i])
        cp.start()
        q_copies.append(cp)
    for p in range(1, NS):
        to = lax.rem(s + p, NS)
        for i, (src, dst) in enumerate(((dq, dqo), (dk, dko), (dv, dvo))):
            cp = remote(
                src.at[rows(to * BLOCK, BLOCK)], dst.at[:, head_spot], qs.at[i, p], qr.at[i, p],
                device(x, y, to),
            )
            cp.start()
            q_copies.append(cp)

    for a in (1, 3, 2, 0):
        for d in (1, 3, 2):
            y_copy(y, d, a).wait_send()
            src = lax.rem(y + NY - d, NY)
            spot = aall.at[src, :, lanes(lax.rem(x + a, NX) * fs, fs)]
            remote(spot, spot, ys.at[d, a], yr.at[d, a], sib).wait_recv()
            if a:
                x_copy(src, d, a).start()
    for b in range(NY):
        gatt[x * NY + b] = aall[b, :, lanes(x * fs, fs)]

    for b in range(NY):
        one = masks[x * NY + b, 0:1, :]
        zero = (1.0 - one.astype(F32)).astype(BF)
        for j in range(width // 128):
            piece = aall[b, :, j * 128 : (j + 1) * 128]
            am[0, b * BLOCK : (b + 1) * BLOCK, j * 128 : (j + 1) * 128] = piece * zero
            am[1, b * BLOCK : (b + 1) * BLOCK, j * 128 : (j + 1) * 128] = piece * one
    load_w.wait()

    step = 256
    pairs = cols // step

    def mix_copy(i, d):
        to = lax.rem(y + d, NY)
        return remote(
            mixp.at[to, :, lanes(i * 128, 128)], mixo.at[:, lanes((i * NY + y) * 128, 128)],
            xs.at[d], xr.at[d], device(x, to, s),
        )

    def mix(t, carry):
        spot = pl.ds(pl.multiple_of(t * step, step), step)
        acc = jnp.dot(am[0], wv[0, :, spot], preferred_element_type=F32)
        acc = acc + jnp.dot(am[1], wv[1, :, spot], preferred_element_type=F32)
        low = acc.astype(BF)
        for b in range(NY):
            mixp[b, :, spot] = low[b * BLOCK : (b + 1) * BLOCK]
        for d in range(1, NY):
            for i in range(step // 128):
                mix_copy(t * (step // 128) + i, d).start()
        return carry

    lax.fori_loop(0, cols // step, mix, 0)
    m_copies = []
    for d in range(1, NY):
        to = lax.rem(y + d, NY)
        m_copies.append(remote(mixp.at[to], mixp.at[to], xs.at[d], xr.at[d], device(x, to, s)))
    for i in range(NZ):
        pltpu.make_async_copy(
            mixp.at[y, :, pl.ds(i * 128, 128)], mixo.at[:, lanes((i * NY + y) * 128, 128)], loc.at[6]
        ).start()
    m_own = pltpu.make_async_copy(mixp.at[y], mixp.at[y], loc.at[6])

    for a in range(1, NX):
        for d in range(NY):
            x_copy(lax.rem(y + NY - d, NY), d, a).wait_send()
            block = gatt.at[lax.rem(x + NX - a, NX) * NY + lax.rem(y + NY - d, NY)]
            remote(block, block, ps.at[d, a], pr.at[d, a], sib).wait_recv()

    def spread(t, carry):
        one = masks[t, 0:1, :]
        zero = (1.0 - one.astype(F32)).astype(BF)
        spot = pl.ds(pl.multiple_of(t * BLOCK, BLOCK), BLOCK)
        for j in range(fs // 128):
            piece = gatt[t, :, j * 128 : (j + 1) * 128].T
            gm[j * 128 : (j + 1) * 128, spot] = piece * zero
            gm[fs + j * 128 : fs + (j + 1) * 128, spot] = piece * one
        return carry

    lax.fori_loop(0, NX * NY, spread, 0)
    for cp in load_go:
        cp.wait()
    on_right.wait()
    on_left.wait()

    def theirs(t, carry):
        spot = pl.ds(pl.multiple_of(lax.rem(lax.div(z, 2) + 1 + t, pairs) * step, step), step)
        for m in range(2):
            lhs = gm[rows(m * fs + (1 - c) * fc, fc), :]
            gws[m, :, spot] = jnp.dot(lhs, gov[:, spot], preferred_element_type=F32).astype(BF)
        remote(gws.at[:, :, spot], gwr.at[:, :, spot], cs.at[t], cr.at[t], sib).start()
        return carry

    def to_plane(i):
        return remote(gwz.at[i], zbuf.at[z], zs.at[i], zr.at[z], device(x, y, 2 * i + c))

    def ours(t, carry):
        pair = lax.rem(lax.div(z, 2) + 1 + t, pairs)
        spot = pl.ds(pl.multiple_of(pair * step, step), step)
        own = []
        for m in range(2):
            lhs = gm[rows(m * fs + c * fc, fc), :]
            own.append(jnp.dot(lhs, gov[:, spot], preferred_element_type=F32))
        remote(gws.at[:, :, spot], gwr.at[:, :, spot], cs.at[t], cr.at[t], sib).wait()
        for m in range(2):
            low = (own[m] + gwr[m, :, spot].astype(F32)).astype(BF)
            for i in range(2):
                gwz[2 * pair + i, m] = low[:, i * 128 : (i + 1) * 128]
        for i in range(2):
            @pl.when(2 * pair + i != z)
            def _():
                to_plane(2 * pair + i).start()
        return carry

    def both(t, carry):
        @pl.when(t < pairs)
        def _():
            theirs(t, 0)

        @pl.when(t > 0)
        def _():
            ours(t - 1, 0)

        return carry

    lax.fori_loop(0, pairs + 1, both, 0)
    for d in range(1, NZ):
        to_plane(lax.rem(z + d, NZ)).wait_send()
        src = lax.rem(z + NZ - d, NZ)
        remote(gwz.at[0], zbuf.at[src], zs.at[0], zr.at[src], sib).wait_recv()
    for m in range(2):
        acc = gwz[z, m].astype(F32)
        for d in range(1, NZ):
            acc = acc + zbuf[lax.rem(z + d, NZ), m].astype(F32)
        for j in range(HALF):
            fin[j, m] = acc[j * 128 : (j + 1) * 128]
    spot = lanes(lax.rem(y, HALF) * 128, 128)
    for j in range(HALF):
        to_y = c * HALF + j
        to_c = lax.div(y, HALF)
        here = jnp.logical_and(to_y == y, to_c == c)
        near = pltpu.make_async_copy(fin.at[j], gwo.at[:, :, spot], loc.at[7])
        far = remote(
            fin.at[j], gwo.at[:, :, spot], fs_.at[j], fr.at[lax.rem(y, HALF)],
            device(x, to_y, 2 * z + to_c),
        )

        @pl.when(here)
        def _():
            near.start()
            near.wait()

        @pl.when(jnp.logical_not(here))
        def _():
            far.start()
            far.wait_send()

    for i in range(HALF):
        from_y = c * HALF + i
        from_c = lax.div(y, HALF)
        here = jnp.logical_and(from_y == y, from_c == c)

        @pl.when(jnp.logical_not(here))
        def _():
            place_ = gwo.at[:, :, pl.ds(i * 128, 128)]
            remote(fin.at[0], place_, fs_.at[0], fr.at[i], sib).wait_recv()

    m_own.wait()
    for cp in m_copies + q_copies:
        cp.wait()


def hbm(n):
    return [pl.BlockSpec(memory_space=pltpu.HBM)] * n


def local(queries, keys, values, w_out, modality, grad_out):
    dma = pltpu.SemaphoreType.DMA
    tokens = queries.shape[1]
    width = queries.shape[2]
    length = tokens * NS
    group = NZ * 128
    shape = jax.ShapeDtypeStruct
    vmem = pl.BlockSpec(memory_space=pltpu.VMEM)
    smem = pl.BlockSpec(memory_space=pltpu.SMEM)
    head = shape((length, HD), BF)
    qh, kh, vh, gah, wg, gog, masks = pl.pallas_call(
        gather_kernel,
        out_shape=(
            head, head, head, head,
            shape((2, width, group), BF),
            shape((NX, NY, BLOCK, group), BF),
            shape((NX * NY, 16, 128), BF),
        ),
        in_specs=[smem] + hbm(5),
        out_specs=tuple(hbm(6) + [vmem]),
        scratch_shapes=[
            pltpu.VMEM((2, width, group), BF),
            pltpu.VMEM((NY, BLOCK, group), BF),
            pltpu.VMEM((2, NY * BLOCK, group), BF),
            pltpu.VMEM((NY, BLOCK, width), BF),
            pltpu.VMEM((NY, BLOCK, width), BF),
            pltpu.VMEM((BLOCK, width), BF),
            pltpu.VMEM((NX * NY, 16, 128), BF),
            dma((8,)),
            dma((3, NS)), dma((3, NS)),
            dma((2, NS)), dma((2, NZ)),
            dma((3, 2)), dma((3, 2)),
            dma((4, 2)), dma((4, 2)),
            dma((NY,)), dma((NY,)),
            dma((NX * NY,)), dma((NX * NY,)),
            dma((8, NY)), dma((8, NY)),
            dma((NS,)), dma((NS,)),
            dma((2,)), dma((2,)),
        ],
        compiler_params=pltpu.CompilerParams(
            collective_id=0, has_side_effects=True, vmem_limit_bytes=40 << 20
        ),
        name="gather",
    )(modality, queries[0], keys[0], values[0], w_out, grad_out[0])

    att, dq, dk, dv = pl.pallas_call(
        attend_kernel,
        out_shape=(head, head, head, head),
        in_specs=[smem] + [vmem] * 4,
        out_specs=(vmem,) * 4,
        scratch_shapes=[
            pltpu.SMEM((length // BLOCK,), jnp.int32),
            pltpu.VMEM((2, length // 256, 256, 256), F32),
            pltpu.VMEM((HD, length), F32),
            pltpu.VMEM((HD, length), F32),
        ],
        compiler_params=pltpu.CompilerParams(vmem_limit_bytes=40 << 20),
        name="attend",
    )(modality, qh, kh, vh, gah)

    fs = width // NX
    all_tokens = NX * NY * BLOCK
    flat = shape((tokens, width), BF)
    mixo, dqo, dko, dvo, gwo = pl.pallas_call(
        project_kernel,
        out_shape=(
            shape((tokens, NY * group), BF), flat, flat, flat,
            shape((2, 128, HALF * 128), F32),
        ),
        in_specs=[pl.BlockSpec(memory_space=pl.ANY)] * 4 + hbm(2) + [vmem],
        out_specs=tuple(hbm(5)),
        scratch_shapes=[
            pltpu.VMEM((NY, BLOCK, width), BF),
            pltpu.VMEM((NX * NY, BLOCK, fs), BF),
            pltpu.VMEM((2, width, group), BF),
            pltpu.VMEM((all_tokens, group), BF),
            pltpu.VMEM((2, NY * BLOCK, width), BF),
            pltpu.VMEM((2 * fs, all_tokens), BF),
            pltpu.VMEM((NY, BLOCK, group), BF),
            pltpu.VMEM((2, fs // 2, group), BF),
            pltpu.VMEM((2, fs // 2, group), BF),
            pltpu.VMEM((NZ, 2, fs // 2, 128), BF),
            pltpu.VMEM((NZ, 2, fs // 2, 128), BF),
            pltpu.VMEM((HALF, 2, 128, 128), F32),
            dma((11,)),
            dma((NS,)), dma((NS,)),
            dma((NY, NX)), dma((NY, NX)),
            dma((NY, NX)), dma((NY, NX)),
            dma((3, NS)), dma((3, NS)),
            dma((NY,)), dma((NY,)),
            dma((group // 256,)), dma((group // 256,)),
            dma((NZ,)), dma((NZ,)),
            dma((HALF,)), dma((HALF,)),
            dma((2,)), dma((2,)),
        ],
        compiler_params=pltpu.CompilerParams(
            collective_id=1, has_side_effects=True, vmem_limit_bytes=52 << 20
        ),
        name="project",
    )(att, dq, dk, dv, wg, gog.reshape(all_tokens, group), masks)
    return mixo[None], dqo[None], dko[None], dvo[None], gwo


def solution(mesh):
    return jax.shard_map(
        local,
        mesh=mesh,
        in_specs=(
            P("dp", "seq", None),
            P("dp", "seq", None),
            P("dp", "seq", None),
            P(None, None, "seq"),
            P("dp", None),
            P("dp", "seq", None),
        ),
        out_specs=(
            P("dp", "seq", None),
            P("dp", "seq", None),
            P("dp", "seq", None),
            P("dp", "seq", None),
            P(None, "dp", "seq"),
        ),
        check_vma=False,
    )
```

```python
import functools
import math

import jax
import jax.numpy as jnp
from jax import lax
from jax.experimental import pallas as pl
from jax.experimental.pallas import tpu as pltpu
from jax.sharding import PartitionSpec as P

HD = 128
BLOCK = 128
NX, NY, NZ = 4, 4, 8
NS = 2 * NZ
HALF = NY // 2
NEG = -1e30
MESH = pl.DeviceIdType.MESH
BF = jnp.bfloat16
F32 = jnp.float32


def place():
    dp = lax.axis_index("dp")
    s = lax.axis_index("seq")
    return lax.div(dp, NY), lax.rem(dp, NY), lax.div(s, 2), lax.rem(s, 2), s


def device(x, y, s):
    return {"dp": x * NY + y, "seq": s}


def lanes(start, size):
    return pl.ds(pl.multiple_of(start, 128), size)


def rows(start, size):
    return pl.ds(pl.multiple_of(start, 128), size)


def remote(src, dst, send, recv, where):
    return pltpu.make_async_remote_copy(
        src_ref=src, dst_ref=dst, send_sem=send, recv_sem=recv, device_id=where, device_id_type=MESH
    )


def enter(x, y, z, c, s, cross):
    barrier = pltpu.get_barrier_semaphore()
    others = [device(x, y, lax.rem(s + p, NS)) for p in range(1, NS)]
    others += [device(lax.rem(x + a, NX), y, s) for a in range(1, NX)]
    others += [device(x, lax.rem(y + b, NY), s) for b in range(1, NY)]
    if cross:
        others += [device(x, lax.rem(y + b, NY), 2 * z + 1 - c) for b in range(1, NY)]
    for other in others:
        pl.semaphore_signal(barrier, inc=1, device_id=other, device_id_type=MESH)
    pl.semaphore_wait(barrier, len(others))


def gather_kernel(
    mod, q, k, v, w, go,
    qh, kh, vh, gah, wg, gog, masks,
    wbuf, gobuf, gom, part, rsbuf, gasum, mbuf,
    loc, qs, qr, ws, wr, xs, xr, cs, cr, gs, gr, ms, mr, ys, yr, hs, hr, os, orr,
):
    x, y, z, c, s = place()
    dp = x * NY + y
    fs = q.shape[1] // NX
    fc = fs // 2
    enter(x, y, z, c, s, False)
    sib = device(x, y, 2 * z + 1 - c)
    left = device(lax.rem(x + NX - 1, NX), y, s)
    right = device(lax.rem(x + 1, NX), y, s)
    xl, xr_, xo = lax.rem(x + NX - 1, NX), lax.rem(x + 1, NX), lax.rem(x + 2, NX)

    def spot(at_x, at_c):
        return rows(at_x * fs + at_c * fc, fc)

    holder = c == lax.div(y, HALF)
    wcols = lanes(lax.rem(y, HALF) * 128, 128)
    zcols = lanes(z * 128, 128)
    w_own = pltpu.make_async_copy(
        w.at[:, spot(x, c), wcols], wbuf.at[:, spot(x, c), zcols], loc.at[0]
    )
    w_sib = remote(
        w.at[:, spot(x, 1 - c), wcols], wbuf.at[:, spot(x, 1 - c), zcols], ws.at[0, 0], wr.at[0, 0], sib
    )

    @pl.when(holder)
    def _():
        w_sib.start()
        w_own.start()

    mbuf[dp] = jnp.full(mbuf.shape[1:], mod[0, s], jnp.int32).astype(F32).astype(BF)
    mask_copies = []
    for d in range(1, NY):
        cp = remote(
            mbuf.at[dp], mbuf.at[dp], ms.at[d], mr.at[d], device(x, lax.rem(y + d, NY), s)
        )
        cp.start()
        mask_copies.append(cp)
    for i in range(NZ):
        pltpu.make_async_copy(
            go.at[:, lanes((i * NY + y) * 128, 128)], gobuf.at[y, :, pl.ds(i * 128, 128)], loc.at[1]
        ).start()
    go_own = pltpu.make_async_copy(gobuf.at[y], gobuf.at[y], loc.at[1])
    go_copies = []
    for d in range(1, NY):
        to = lax.rem(y + d, NY)
        for i in range(NZ):
            remote(
                go.at[:, lanes((i * NY + to) * 128, 128)], gobuf.at[y, :, pl.ds(i * 128, 128)],
                gs.at[d], gr.at[d], device(x, to, s),
            ).start()
        src = lax.rem(y + NY - d, NY)
        go_copies.append(remote(gobuf.at[y], gobuf.at[src], gs.at[d], gr.at[d], device(x, to, s)))

    sent = []
    up, down = device(x, y, lax.rem(s + 2, NS)), device(x, y, lax.rem(s + NS - 2, NS))
    last = NZ // 2

    def chunk(k):
        t = (k + 1) // 2
        return lanes(lax.rem(z + NZ - t if k % 2 else z + t, NZ) * 128, 128)

    def start(cp):
        cp.start()
        sent.append(cp)

    def block(at_x, at_c, k, m=None):
        return wbuf.at[slice(None) if m is None else m, spot(at_x, at_c), chunk(k)]

    def along_z(t):
        m = (0, 1) if t == last else (None, None)
        first, second = (0, 0) if t == 1 else (2 * t - 3, 2 * t - 2)
        here = block(x, c, first, m[0])
        start(remote(here, here, ws.at[0, t], wr.at[0, t], up))
        here = block(x, c, second, m[1])
        start(remote(here, here, ws.at[1, t], wr.at[1, t], down))

    def from_z(t):
        first, second = (2 * t - 1, 2 * t) if t < last else (NZ - 1, NZ - 1)
        m = (0, 1) if t == last else (None, None)
        here = block(x, c, first, m[0])
        remote(here, here, ws.at[0, t], wr.at[0, t], sib).wait_recv()
        here = block(x, c, second, m[1])
        remote(here, here, ws.at[1, t], wr.at[1, t], sib).wait_recv()

    def spread_x(k):
        here = block(x, c, k)
        start(remote(here, here, xs.at[0, k], xr.at[0, k], right))
        start(remote(here, here, xs.at[1, k], xr.at[1, k], left))
        start(remote(here, here, cs.at[0, k], cr.at[0, k], sib))

    def from_x(k):
        here = block(xl, c, k)
        remote(here, here, xs.at[0, k], xr.at[0, k], sib).wait_recv()
        half = block(xl, c, k, 0)
        start(remote(half, half, xs.at[2, k], xr.at[2, k], right))
        start(remote(here, here, cs.at[1, k], cr.at[1, k], sib))
        here = block(xr_, c, k)
        remote(here, here, xs.at[1, k], xr.at[1, k], sib).wait_recv()
        half = block(xr_, c, k, 1)
        start(remote(half, half, xs.at[3, k], xr.at[3, k], left))
        start(remote(here, here, cs.at[2, k], cr.at[2, k], sib))

    def from_two(k):
        for m in range(2):
            half = block(xo, c, k, m)
            remote(half, half, xs.at[2 + m, k], xr.at[2 + m, k], sib).wait_recv()
        here = block(xo, c, k)
        start(remote(here, here, cs.at[3, k], cr.at[3, k], sib))

    def other_core(i, at_x):
        for k in range(NZ):
            here = block(at_x, 1 - c, k)
            remote(here, here, cs.at[i, k], cr.at[i, k], sib).wait_recv()

    @pl.when(holder)
    def _():
        w_own.wait()

    @pl.when(jnp.logical_not(holder))
    def _():
        here = wbuf.at[:, spot(x, c), zcols]
        remote(here, here, ws.at[0, 0], wr.at[0, 0], sib).wait_recv()

    along_z(1)
    spread_x(0)
    for t in range(1, last):
        from_z(t)
        along_z(t + 1)
        spread_x(2 * t - 1)
        spread_x(2 * t)
        for n in ((0,) if t == 1 else (2 * t - 3, 2 * t - 2)):
            from_x(n)
    from_z(last)
    spread_x(NZ - 1)

    token_spot = rows(s * BLOCK, BLOCK)
    qkv_copies = []
    for i, (src, dst) in enumerate(((q, qh), (k, kh), (v, vh))):
        cp = pltpu.make_async_copy(src.at[:, lanes(s * HD, HD)], dst.at[token_spot], loc.at[2 + i])
        cp.start()
        qkv_copies.append(cp)
    for p in range(1, NS):
        to = lax.rem(s + p, NS)
        for i, (src, dst) in enumerate(((q, qh), (k, kh), (v, vh))):
            cp = remote(
                src.at[:, lanes(to * HD, HD)], dst.at[token_spot],
                qs.at[i, p], qr.at[i, p], device(x, y, to),
            )
            cp.start()
            qkv_copies.append(cp)

    go_own.wait()
    for cp in go_copies:
        cp.wait()
    gog_own = pltpu.make_async_copy(gobuf, gog.at[x], loc.at[5])
    gog_own.start()
    for d in range(1, NY):
        here = mbuf.at[x * NY + lax.rem(y + NY - d, NY)]
        mask_copies[d - 1].wait_send()
        remote(here, here, ms.at[d], mr.at[d], sib).wait_recv()
    mask_copies = []
    for a in range(1, NX):
        here = mbuf.at[pl.ds(x * NY, NY)]
        cp = remote(here, here, ms.at[NY + a], mr.at[NY + a], device(lax.rem(x + a, NX), y, s))
        cp.start()
        mask_copies.append(cp)
    for b in range(NY):
        one = mbuf[x * NY + b, 0:1, :]
        zero = (1.0 - one.astype(F32)).astype(BF)
        for j in range(NZ):
            piece = gobuf[b, :, j * 128 : (j + 1) * 128]
            gom[0, b * BLOCK : (b + 1) * BLOCK, j * 128 : (j + 1) * 128] = piece * zero
            gom[1, b * BLOCK : (b + 1) * BLOCK, j * 128 : (j + 1) * 128] = piece * one
    y_copies = {}

    def compute(step, at_x, at_c):
        f = at_x * 2 + at_c
        part_rows = spot(at_x, at_c)
        cols = lanes(f * fc, fc)
        acc = lax.dot_general(
            gom[0], wbuf[0, part_rows, :], (((1,), (1,)), ((), ())), preferred_element_type=F32
        ) + lax.dot_general(
            gom[1], wbuf[1, part_rows, :], (((1,), (1,)), ((), ())), preferred_element_type=F32
        )
        low = acc.astype(BF)
        for b in range(NY):
            part[b, :, cols] = low[b * BLOCK : (b + 1) * BLOCK]
        y_copies[step] = []
        for d in range(1, NY):
            to = lax.rem(y + d, NY)
            cp = remote(
                part.at[to, :, cols], rsbuf.at[y, :, cols], ys.at[step, d], yr.at[step, d],
                device(x, to, s),
            )
            cp.start()
            y_copies[step].append(cp)

    def head_copies(at_x, at_c, h):
        f = at_x * 2 + at_c
        heads = fc // HD
        head = f * heads + h
        src = gasum.at[:, lanes(head * HD, HD)]
        far = remote(src, gah.at[token_spot], hs.at[head], hr.at[s], device(x, y, head))
        near = pltpu.make_async_copy(src, gah.at[token_spot], loc.at[6])
        return head, far, near

    def total(step, at_x, at_c):
        f = at_x * 2 + at_c
        cols = lanes(f * fc, fc)
        for cp in y_copies[step]:
            cp.wait()
        acc = part[y, :, cols].astype(F32)
        for d in range(1, NY):
            acc = acc + rsbuf[lax.rem(y + d, NY), :, cols].astype(F32)
        gasum[:, cols] = acc.astype(BF)
        for h in range(fc // HD):
            head, far, near = head_copies(at_x, at_c, h)

            @pl.when(head == s)
            def _():
                near.start()

            @pl.when(head != s)
            def _():
                far.start()

    order = [(x, c), (x, 1 - c), (xl, c), (xl, 1 - c), (xr_, c), (xr_, 1 - c), (xo, c), (xo, 1 - c)]
    from_two(0)
    compute(0, *order[0])
    for n in (NZ - 3, NZ - 2):
        from_x(n)
    for n in (1, 2):
        from_two(n)
    other_core(0, x)
    compute(1, *order[1])
    from_x(NZ - 1)
    total(0, *order[0])
    compute(2, *order[2])
    for n in (3, 4):
        from_two(n)
    compute(4, *order[4])
    total(1, *order[1])
    other_core(1, xl)
    compute(3, *order[3])
    total(2, *order[2])
    other_core(2, xr_)
    compute(5, *order[5])
    total(4, *order[4])
    for n in (5, 6, 7):
        from_two(n)
    total(3, *order[3])
    total(5, *order[5])

    gog_own.wait()
    go_right = remote(gobuf, gog.at[x], os.at[0], orr.at[0], right)
    go_left = remote(gobuf, gog.at[x], os.at[1], orr.at[1], left)
    go_right.start()
    go_left.start()

    compute(6, *order[6])
    other_core(3, xo)
    compute(7, *order[7])
    keep = pltpu.make_async_copy(wbuf, wg, loc.at[7])
    keep.start()
    total(6, *order[6])
    total(7, *order[7])

    for step in range(8):
        for h in range(fc // HD):
            head, far, near = head_copies(*order[step], h)

            @pl.when(head == s)
            def _():
                near.wait()

            @pl.when(head != s)
            def _():
                far.wait_send()

    for p in range(1, NS):
        src = lax.rem(s + NS - p, NS)
        here = gah.at[rows(src * BLOCK, BLOCK)]
        remote(here, here, hs.at[0], hr.at[src], sib).wait_recv()
    for cp in qkv_copies:
        cp.wait()

    @pl.when(holder)
    def _():
        w_sib.wait_send()

    for cp in sent:
        cp.wait_send()
    for a in range(1, NX):
        here = mbuf.at[pl.ds(lax.rem(x + NX - a, NX) * NY, NY)]
        mask_copies[a - 1].wait_send()
        remote(here, here, ms.at[NY + a], mr.at[NY + a], sib).wait_recv()
    masks[...] = mbuf[...]
    go_right.wait()
    go_left.wait()
    keep.wait()


def attend_kernel(
    mod, q_in, k_in, v_in, ga_in, att_out, dq_out, dk_out, dv_out,
    end, s_buf, dk_t, dv_t, q, k, v, ga, att, dq, dk, dv, ins, outs,
):
    length = q.shape[0]
    loads = []
    for i, (src, dst) in enumerate(((q_in, q), (k_in, k), (v_in, v), (ga_in, ga))):
        cp = pltpu.make_async_copy(src, dst, ins.at[i])
        cp.start()
        loads.append(cp)
    stores = []

    def store(i, src, dst, at):
        cp = pltpu.make_async_copy(src.at[at], dst.at[at], outs.at[i, at.start // at.size])
        cp.start()
        stores.append(cp)

    blocks = length // BLOCK
    qb = 4 * BLOCK
    kb = 2 * BLOCK
    strips = length // qb
    scale = HD ** -0.5
    c2 = scale * math.log2(math.e)
    end[blocks - 1] = length
    for b in range(blocks - 2, -1, -1):
        end[b] = jnp.where(mod[0, b + 1] == 1, end[b + 1], (b + 1) * BLOCK)
    dk_t[...] = jnp.zeros_like(dk_t)
    dv_t[...] = jnp.zeros_like(dv_t)
    nt = (((1,), (1,)), ((), ()))
    row = lax.broadcasted_iota(jnp.int32, (qb, 1), 0)

    loads[0].wait()
    loads[1].wait()
    for i in range(strips):
        q_rows = pl.ds(i * qb, qb)
        buf = s_buf.at[i % 2]
        qi = q[q_rows, :]
        limit, most = row + (i * qb + 1), (i + 1) * qb
        for b in range(qb // BLOCK):
            at = i * (qb // BLOCK) + b
            reach = jnp.where(mod[0, at] == 1, end[at], 0)
            most = jnp.maximum(most, reach)
            inside = jnp.logical_and(row >= b * BLOCK, row < (b + 1) * BLOCK)
            limit = jnp.where(inside, jnp.maximum(limit, reach), limit)
        fixed = -(-(i + 1) * qb // kb)
        n = lax.div(most + (kb - 1), kb)

        def part(j):
            return pl.ds(j * kb if isinstance(j, int) else pl.multiple_of(j * kb, kb), kb)

        def chunks(body, carry):
            for j in range(fixed):
                carry = body(j, carry)
            if fixed * kb < length:
                carry = lax.fori_loop(fixed, n, body, carry)
            return carry

        def scores(j, m):
            sc = lax.dot_general(qi, k[part(j), :], nt, preferred_element_type=F32)
            if not isinstance(j, int) or (j + 1) * kb > i * qb:
                col = lax.broadcasted_iota(jnp.int32, (qb, kb), 1) + j * kb
                sc = jnp.where(col < limit, sc, NEG)
            buf[j] = sc
            for t in range(kb // 128):
                m = jnp.maximum(m, sc[:, t * 128 : (t + 1) * 128])
            return m

        m = chunks(scores, jnp.full((qb, 128), NEG, F32))
        m = jnp.max(m, axis=1, keepdims=True)

        if i == 0:
            loads[2].wait()
            loads[3].wait()
        gi = ga[q_rows, :].astype(F32)

        def forward(j, carry):
            total, acc = carry
            e = jnp.exp2((buf[j] - m) * c2)
            buf[j] = e
            for t in range(kb // 128):
                total = total + e[:, t * 128 : (t + 1) * 128]
            return total, acc + jnp.dot(e.astype(BF), v[part(j), :], preferred_element_type=F32)

        total, acc = chunks(forward, (jnp.zeros((qb, 128), F32), jnp.zeros((qb, HD), F32)))
        inv = 1.0 / jnp.sum(total, axis=1, keepdims=True)
        out = (acc * inv).astype(BF)
        att[q_rows, :] = out
        store(0, att, att_out, q_rows)
        gl = gi * inv
        delta = jnp.sum(gl * out.astype(F32), axis=1, keepdims=True)
        gl = gl.astype(BF)
        gt = gl.T
        qt = qi.T

        def backward(j, acc):
            e = buf[j]
            dp = lax.dot_general(gl, v[part(j), :], nt, preferred_element_type=F32)
            ds = (e * (dp - delta)).astype(BF)
            dv_t[:, part(j)] += jnp.dot(gt, e.astype(BF), preferred_element_type=F32)
            dk_t[:, part(j)] += jnp.dot(qt, ds, preferred_element_type=F32)
            return acc + jnp.dot(ds, k[part(j), :], preferred_element_type=F32)

        acc = chunks(backward, jnp.zeros((qb, HD), F32))
        dq[q_rows, :] = (acc * scale).astype(BF)
        store(1, dq, dq_out, q_rows)

    for i in range(strips):
        spot = pl.ds(i * qb, qb)
        dk[spot, :] = (dk_t[:, spot].T * scale).astype(BF)
        dv[spot, :] = dv_t[:, spot].T.astype(BF)
        store(2, dk, dk_out, spot)
        store(3, dv, dv_out, spot)
    for cp in stores:
        cp.wait()


def project_kernel(
    att, dq, dk, dv, wg, gog, masks,
    mixo, dqo, dko, dvo, gwo,
    aall, gatt, wv, gov, am, gm, mixp, gws, gwr, gwz, zbuf, fin,
    loc, hs, hr, ps, pr, ys, yr, qs, qr, xs, xr, cs, cr, zs, zr, fs_, fr, os, orr,
):
    x, y, z, c, s = place()
    width = wg.shape[1]
    fs = width // NX
    fc = fs // 2
    cols = wg.shape[2]
    tokens = NX * NY * BLOCK
    enter(x, y, z, c, s, True)
    sib = device(x, y, 2 * z + 1 - c)

    head_spot = lanes(s * HD, HD)
    a_own = pltpu.make_async_copy(att.at[rows(s * BLOCK, BLOCK)], aall.at[y, :, head_spot], loc.at[0])
    a_own.start()
    a_copies = []
    for p in range(1, NS):
        to = lax.rem(s + p, NS)
        cp = remote(
            att.at[rows(to * BLOCK, BLOCK)], aall.at[y, :, head_spot], hs.at[p], hr.at[p],
            device(x, y, to),
        )
        cp.start()
        a_copies.append(cp)
    xl, xo, xr_ = lax.rem(x + NX - 1, NX), lax.rem(x + 2, NX), lax.rem(x + 1, NX)
    left, right = device(xl, y, s), device(xr_, y, s)
    half = HALF * BLOCK

    def go_part(at_x, h):
        return pl.ds(pl.multiple_of(at_x * (NY * BLOCK) + h * half, half), half)

    on_right = remote(gog.at[go_part(xl, 0)], gov.at[go_part(xl, 0)], os.at[0], orr.at[0], right)
    on_left = remote(gog.at[go_part(xr_, 1)], gov.at[go_part(xr_, 1)], os.at[1], orr.at[1], left)
    on_right.start()
    on_left.start()
    load_go = []
    for i, at_x in enumerate((x, xl, xr_)):
        spot = pl.ds(pl.multiple_of(at_x * (NY * BLOCK), NY * BLOCK), NY * BLOCK)
        cp = pltpu.make_async_copy(gog.at[spot], gov.at[spot], loc.at[8 + i])
        cp.start()
        load_go.append(cp)
    load_w = pltpu.make_async_copy(wg, wv, loc.at[2])
    load_w.start()
    a_own.wait()
    for cp in a_copies:
        cp.wait()

    def y_copy(block, d, a):
        spot = aall.at[block, :, lanes(lax.rem(x + a, NX) * fs, fs)]
        return remote(spot, spot, ys.at[d, a], yr.at[d, a], device(x, lax.rem(y + d, NY), s))

    def x_copy(block, d, a):
        to_x = lax.rem(x + a, NX)
        return remote(
            aall.at[block, :, lanes(to_x * fs, fs)], gatt.at[x * NY + block],
            ps.at[d, a], pr.at[d, a], device(to_x, y, s),
        )

    for a in (1, 3, 2):
        for d in (1, 3, 2):
            y_copy(y, d, a).start()
        x_copy(y, 0, a).start()
    for d in (1, 3, 2):
        y_copy(y, d, 0).start()
    q_copies = []
    for i, (src, dst) in enumerate(((dq, dqo), (dk, dko), (dv, dvo))):
        cp = pltpu.make_async_copy(src.at[rows(s * BLOCK, BLOCK)], dst.at[:, head_spot], loc.at[3 + i])
        cp.start()
        q_copies.append(cp)
    for p in range(1, NS):
        to = lax.rem(s + p, NS)
        for i, (src, dst) in enumerate(((dq, dqo), (dk, dko), (dv, dvo))):
            cp = remote(
                src.at[rows(to * BLOCK, BLOCK)], dst.at[:, head_spot], qs.at[i, p], qr.at[i, p],
                device(x, y, to),
            )
            cp.start()
            q_copies.append(cp)

    for a in (1, 3, 2, 0):
        for d in (1, 3, 2):
            y_copy(y, d, a).wait_send()
            src = lax.rem(y + NY - d, NY)
            spot = aall.at[src, :, lanes(lax.rem(x + a, NX) * fs, fs)]
            remote(spot, spot, ys.at[d, a], yr.at[d, a], sib).wait_recv()
            if a:
                x_copy(src, d, a).start()
    for b in range(NY):
        gatt[x * NY + b] = aall[b, :, lanes(x * fs, fs)]

    step = 256
    pairs = cols // step

    for a in range(1, NX):
        for d in range(NY):
            x_copy(lax.rem(y + NY - d, NY), d, a).wait_send()
            block = gatt.at[lax.rem(x + NX - a, NX) * NY + lax.rem(y + NY - d, NY)]
            remote(block, block, ps.at[d, a], pr.at[d, a], sib).wait_recv()

    def spread(t, carry):
        one = masks[t, 0:1, :]
        zero = (1.0 - one.astype(F32)).astype(BF)
        spot = pl.ds(pl.multiple_of(t * BLOCK, BLOCK), BLOCK)
        for j in range(fs // 128):
            piece = gatt[t, :, j * 128 : (j + 1) * 128].T
            gm[j * 128 : (j + 1) * 128, spot] = piece * zero
            gm[fs + j * 128 : fs + (j + 1) * 128, spot] = piece * one
        return carry

    lax.fori_loop(0, NX * NY, spread, 0)
    for cp in load_go:
        cp.wait()
    on_right.wait()
    on_left.wait()

    def theirs(t, carry):
        spot = pl.ds(pl.multiple_of(lax.rem(lax.div(z, 2) + 1 + t, pairs) * step, step), step)
        for m in range(2):
            lhs = gm[rows(m * fs + (1 - c) * fc, fc), :]
            gws[m, :, spot] = jnp.dot(lhs, gov[:, spot], preferred_element_type=F32).astype(BF)
        remote(gws.at[:, :, spot], gwr.at[:, :, spot], cs.at[t], cr.at[t], sib).start()
        return carry

    def to_plane(i):
        return remote(gwz.at[i], zbuf.at[z], zs.at[i], zr.at[z], device(x, y, 2 * i + c))

    def ours(t, carry):
        pair = lax.rem(lax.div(z, 2) + 1 + t, pairs)
        spot = pl.ds(pl.multiple_of(pair * step, step), step)
        own = []
        for m in range(2):
            lhs = gm[rows(m * fs + c * fc, fc), :]
            own.append(jnp.dot(lhs, gov[:, spot], preferred_element_type=F32))
        remote(gws.at[:, :, spot], gwr.at[:, :, spot], cs.at[t], cr.at[t], sib).wait()
        for m in range(2):
            low = (own[m] + gwr[m, :, spot].astype(F32)).astype(BF)
            for i in range(2):
                gwz[2 * pair + i, m] = low[:, i * 128 : (i + 1) * 128]
        for i in range(2):
            @pl.when(2 * pair + i != z)
            def _():
                to_plane(2 * pair + i).start()
        return carry

    def both(t, carry):
        @pl.when(t < pairs)
        def _():
            theirs(t, 0)

        @pl.when(t > 0)
        def _():
            ours(t - 1, 0)

        return carry

    lax.fori_loop(0, pairs + 1, both, 0)
    for b in range(NY):
        one = masks[x * NY + b, 0:1, :]
        zero = (1.0 - one.astype(F32)).astype(BF)
        for j in range(width // 128):
            piece = aall[b, :, j * 128 : (j + 1) * 128]
            am[0, b * BLOCK : (b + 1) * BLOCK, j * 128 : (j + 1) * 128] = piece * zero
            am[1, b * BLOCK : (b + 1) * BLOCK, j * 128 : (j + 1) * 128] = piece * one
    load_w.wait()

    def mix_copy(i, d):
        to = lax.rem(y + d, NY)
        return remote(
            mixp.at[to, :, lanes(i * 128, 128)], mixo.at[:, lanes((i * NY + y) * 128, 128)],
            xs.at[d], xr.at[d], device(x, to, s),
        )

    def mix(t, carry):
        spot = pl.ds(pl.multiple_of(t * step, step), step)
        acc = jnp.dot(am[0], wv[0, :, spot], preferred_element_type=F32)
        acc = acc + jnp.dot(am[1], wv[1, :, spot], preferred_element_type=F32)
        low = acc.astype(BF)
        for b in range(NY):
            mixp[b, :, spot] = low[b * BLOCK : (b + 1) * BLOCK]
        for d in range(1, NY):
            for i in range(step // 128):
                mix_copy(t * (step // 128) + i, d).start()
        return carry

    lax.fori_loop(0, cols // step, mix, 0)
    m_copies = []
    for d in range(1, NY):
        to = lax.rem(y + d, NY)
        m_copies.append(remote(mixp.at[to], mixp.at[to], xs.at[d], xr.at[d], device(x, to, s)))
    for i in range(NZ):
        pltpu.make_async_copy(
            mixp.at[y, :, pl.ds(i * 128, 128)], mixo.at[:, lanes((i * NY + y) * 128, 128)], loc.at[6]
        ).start()
    m_own = pltpu.make_async_copy(mixp.at[y], mixp.at[y], loc.at[6])

    for d in range(1, NZ):
        to_plane(lax.rem(z + d, NZ)).wait_send()
        src = lax.rem(z + NZ - d, NZ)
        remote(gwz.at[0], zbuf.at[src], zs.at[0], zr.at[src], sib).wait_recv()
    for m in range(2):
        acc = gwz[z, m].astype(F32)
        for d in range(1, NZ):
            acc = acc + zbuf[lax.rem(z + d, NZ), m].astype(F32)
        for j in range(HALF):
            fin[j, m] = acc[j * 128 : (j + 1) * 128]
    spot = lanes(lax.rem(y, HALF) * 128, 128)
    for j in range(HALF):
        to_y = c * HALF + j
        to_c = lax.div(y, HALF)
        here = jnp.logical_and(to_y == y, to_c == c)
        near = pltpu.make_async_copy(fin.at[j], gwo.at[:, :, spot], loc.at[7])
        far = remote(
            fin.at[j], gwo.at[:, :, spot], fs_.at[j], fr.at[lax.rem(y, HALF)],
            device(x, to_y, 2 * z + to_c),
        )

        @pl.when(here)
        def _():
            near.start()
            near.wait()

        @pl.when(jnp.logical_not(here))
        def _():
            far.start()
            far.wait_send()

    for i in range(HALF):
        from_y = c * HALF + i
        from_c = lax.div(y, HALF)
        here = jnp.logical_and(from_y == y, from_c == c)

        @pl.when(jnp.logical_not(here))
        def _():
            place_ = gwo.at[:, :, pl.ds(i * 128, 128)]
            remote(fin.at[0], place_, fs_.at[0], fr.at[i], sib).wait_recv()

    m_own.wait()
    for cp in m_copies + q_copies:
        cp.wait()


def finish_kernel(*refs):
    sources, results, staged, sems = refs[:5], refs[5:10], refs[10:15], refs[15]
    loads = [pltpu.make_async_copy(sources[i], staged[i], sems.at[0, i]) for i in range(5)]
    stores = [pltpu.make_async_copy(staged[i], results[i], sems.at[1, i]) for i in range(5)]
    for cp in loads:
        cp.start()
    for load, cp in zip(loads, stores):
        load.wait()
        cp.start()
    for cp in stores:
        cp.wait()


def hbm(n):
    return [pl.BlockSpec(memory_space=pltpu.HBM)] * n


def local(queries, keys, values, w_out, modality, grad_out):
    dma = pltpu.SemaphoreType.DMA
    tokens = queries.shape[1]
    width = queries.shape[2]
    length = tokens * NS
    group = NZ * 128
    shape = jax.ShapeDtypeStruct
    vmem = pl.BlockSpec(memory_space=pltpu.VMEM)
    smem = pl.BlockSpec(memory_space=pltpu.SMEM)
    head = shape((length, HD), BF)
    qh, kh, vh, gah, wg, gog, masks = pl.pallas_call(
        gather_kernel,
        out_shape=(
            head, head, head, head,
            shape((2, width, group), BF),
            shape((NX, NY, BLOCK, group), BF),
            shape((NX * NY, 16, 128), BF),
        ),
        in_specs=[smem] + hbm(5),
        out_specs=tuple(hbm(6) + [vmem]),
        scratch_shapes=[
            pltpu.VMEM((2, width, group), BF),
            pltpu.VMEM((NY, BLOCK, group), BF),
            pltpu.VMEM((2, NY * BLOCK, group), BF),
            pltpu.VMEM((NY, BLOCK, width), BF),
            pltpu.VMEM((NY, BLOCK, width), BF),
            pltpu.VMEM((BLOCK, width), BF),
            pltpu.VMEM((NX * NY, 16, 128), BF),
            dma((8,)),
            dma((3, NS)), dma((3, NS)),
            dma((2, NZ)), dma((2, NZ)),
            dma((4, NZ)), dma((4, NZ)),
            dma((4, NZ)), dma((4, NZ)),
            dma((NY,)), dma((NY,)),
            dma((NX * NY,)), dma((NX * NY,)),
            dma((8, NY)), dma((8, NY)),
            dma((NS,)), dma((NS,)),
            dma((2,)), dma((2,)),
        ],
        compiler_params=pltpu.CompilerParams(
            collective_id=0, has_side_effects=True, vmem_limit_bytes=40 << 20
        ),
        name="gather",
    )(modality, queries[0], keys[0], values[0], w_out, grad_out[0])

    att, dq, dk, dv = pl.pallas_call(
        attend_kernel,
        out_shape=(head, head, head, head),
        in_specs=[smem] + hbm(4),
        out_specs=tuple(hbm(4)),
        scratch_shapes=[
            pltpu.SMEM((length // BLOCK,), jnp.int32),
            pltpu.VMEM((2, length // 256, 512, 256), F32),
            pltpu.VMEM((HD, length), F32),
            pltpu.VMEM((HD, length), F32),
        ]
        + [pltpu.VMEM((length, HD), BF)] * 8
        + [dma((4,)), dma((4, length // 256))],
        compiler_params=pltpu.CompilerParams(vmem_limit_bytes=40 << 20),
        name="attend",
    )(modality, qh, kh, vh, gah)

    fs = width // NX
    all_tokens = NX * NY * BLOCK
    flat = shape((tokens, width), BF)
    mixo, dqo, dko, dvo, gwo = pl.pallas_call(
        project_kernel,
        out_shape=(
            shape((tokens, NY * group), BF), flat, flat, flat,
            shape((2, 128, HALF * 128), F32),
        ),
        in_specs=hbm(6) + [vmem],
        out_specs=tuple(hbm(5)),
        scratch_shapes=[
            pltpu.VMEM((NY, BLOCK, width), BF),
            pltpu.VMEM((NX * NY, BLOCK, fs), BF),
            pltpu.VMEM((2, width, group), BF),
            pltpu.VMEM((all_tokens, group), BF),
            pltpu.VMEM((2, NY * BLOCK, width), BF),
            pltpu.VMEM((2 * fs, all_tokens), BF),
            pltpu.VMEM((NY, BLOCK, group), BF),
            pltpu.VMEM((2, fs // 2, group), BF),
            pltpu.VMEM((2, fs // 2, group), BF),
            pltpu.VMEM((NZ, 2, fs // 2, 128), BF),
            pltpu.VMEM((NZ, 2, fs // 2, 128), BF),
            pltpu.VMEM((HALF, 2, 128, 128), F32),
            dma((11,)),
            dma((NS,)), dma((NS,)),
            dma((NY, NX)), dma((NY, NX)),
            dma((NY, NX)), dma((NY, NX)),
            dma((3, NS)), dma((3, NS)),
            dma((NY,)), dma((NY,)),
            dma((group // 256,)), dma((group // 256,)),
            dma((NZ,)), dma((NZ,)),
            dma((HALF,)), dma((HALF,)),
            dma((2,)), dma((2,)),
        ],
        compiler_params=pltpu.CompilerParams(
            collective_id=1, has_side_effects=True, vmem_limit_bytes=52 << 20
        ),
        name="project",
    )(att, dq, dk, dv, wg, gog.reshape(all_tokens, group), masks)
    mixed, dq, dk, dv, gw = pl.pallas_call(
            finish_kernel,
            out_shape=tuple(shape(a.shape, a.dtype) for a in (mixo, dqo, dko, dvo, gwo)),
            in_specs=hbm(5),
            out_specs=tuple(hbm(5)),
            scratch_shapes=[pltpu.VMEM(a.shape, a.dtype) for a in (mixo, dqo, dko, dvo, gwo)]
            + [dma((2, 5))],
            name="finish",
        )(mixo, dqo, dko, dvo, gwo)
    return mixed[None], dq[None], dk[None], dv[None], gw


def solution(mesh):
    return jax.shard_map(
        local,
        mesh=mesh,
        in_specs=(
            P("dp", "seq", None),
            P("dp", "seq", None),
            P("dp", "seq", None),
            P(None, None, "seq"),
            P("dp", None),
            P("dp", "seq", None),
        ),
        out_specs=(
            P("dp", "seq", None),
            P("dp", "seq", None),
            P("dp", "seq", None),
            P("dp", "seq", None),
            P(None, "dp", "seq"),
        ),
        check_vma=False,
    )
```

```python
import functools
import math

import jax
import jax.numpy as jnp
from jax import lax
from jax.experimental import pallas as pl
from jax.experimental.pallas import tpu as pltpu
from jax.sharding import PartitionSpec as P

HD = 128
BLOCK = 128
NX, NY, NZ = 4, 4, 8
NS = 2 * NZ
HALF = NY // 2
NEG = -1e30
MESH = pl.DeviceIdType.MESH
BF = jnp.bfloat16
F32 = jnp.float32


def place():
    dp = lax.axis_index("dp")
    s = lax.axis_index("seq")
    return lax.div(dp, NY), lax.rem(dp, NY), lax.div(s, 2), lax.rem(s, 2), s


def device(x, y, s):
    return {"dp": x * NY + y, "seq": s}


def lanes(start, size):
    return pl.ds(pl.multiple_of(start, 128), size)


def rows(start, size):
    return pl.ds(pl.multiple_of(start, 128), size)


def remote(src, dst, send, recv, where):
    return pltpu.make_async_remote_copy(
        src_ref=src, dst_ref=dst, send_sem=send, recv_sem=recv, device_id=where, device_id_type=MESH
    )


def enter(x, y, z, c, s, cross):
    barrier = pltpu.get_barrier_semaphore()
    others = [device(x, y, lax.rem(s + p, NS)) for p in range(1, NS)]
    others += [device(lax.rem(x + a, NX), y, s) for a in range(1, NX)]
    others += [device(x, lax.rem(y + b, NY), s) for b in range(1, NY)]
    if cross:
        others += [device(x, lax.rem(y + b, NY), 2 * z + 1 - c) for b in range(1, NY)]
    for other in others:
        pl.semaphore_signal(barrier, inc=1, device_id=other, device_id_type=MESH)
    pl.semaphore_wait(barrier, len(others))


def gather_kernel(
    mod, q, k, v, w, go,
    qh, kh, vh, gah, wg, gog, masks,
    wbuf, gobuf, gom, part, rsbuf, gasum, mbuf,
    loc, qs, qr, ws, wr, xs, xr, cs, cr, gs, gr, ms, mr, ys, yr, hs, hr, os, orr,
):
    x, y, z, c, s = place()
    dp = x * NY + y
    fs = q.shape[1] // NX
    fc = fs // 2
    enter(x, y, z, c, s, False)
    sib = device(x, y, 2 * z + 1 - c)
    left = device(lax.rem(x + NX - 1, NX), y, s)
    right = device(lax.rem(x + 1, NX), y, s)
    xl, xr_, xo = lax.rem(x + NX - 1, NX), lax.rem(x + 1, NX), lax.rem(x + 2, NX)

    def spot(at_x, at_c):
        return rows(at_x * fs + at_c * fc, fc)

    holder = c == lax.div(y, HALF)
    wcols = lanes(lax.rem(y, HALF) * 128, 128)
    zcols = lanes(z * 128, 128)
    w_own = pltpu.make_async_copy(
        w.at[:, spot(x, c), wcols], wbuf.at[:, spot(x, c), zcols], loc.at[0]
    )
    w_sib = remote(
        w.at[:, spot(x, 1 - c), wcols], wbuf.at[:, spot(x, 1 - c), zcols], ws.at[0, 0], wr.at[0, 0], sib
    )

    @pl.when(holder)
    def _():
        w_sib.start()
        w_own.start()

    mbuf[dp] = jnp.full(mbuf.shape[1:], mod[0, s], jnp.int32).astype(F32).astype(BF)
    mask_copies = []
    for d in range(1, NY):
        cp = remote(
            mbuf.at[dp], mbuf.at[dp], ms.at[d], mr.at[d], device(x, lax.rem(y + d, NY), s)
        )
        cp.start()
        mask_copies.append(cp)
    for i in range(NZ):
        pltpu.make_async_copy(
            go.at[:, lanes((i * NY + y) * 128, 128)], gobuf.at[y, :, pl.ds(i * 128, 128)], loc.at[1]
        ).start()
    go_own = pltpu.make_async_copy(gobuf.at[y], gobuf.at[y], loc.at[1])
    go_copies = []
    for d in range(1, NY):
        to = lax.rem(y + d, NY)
        for i in range(NZ):
            remote(
                go.at[:, lanes((i * NY + to) * 128, 128)], gobuf.at[y, :, pl.ds(i * 128, 128)],
                gs.at[d], gr.at[d], device(x, to, s),
            ).start()
        src = lax.rem(y + NY - d, NY)
        go_copies.append(remote(gobuf.at[y], gobuf.at[src], gs.at[d], gr.at[d], device(x, to, s)))

    sent = []
    up, down = device(x, y, lax.rem(s + 2, NS)), device(x, y, lax.rem(s + NS - 2, NS))
    last = NZ // 2

    def chunk(k):
        t = (k + 1) // 2
        return lanes(lax.rem(z + NZ - t if k % 2 else z + t, NZ) * 128, 128)

    def start(cp):
        cp.start()
        sent.append(cp)

    def block(at_x, at_c, k, m=None):
        return wbuf.at[slice(None) if m is None else m, spot(at_x, at_c), chunk(k)]

    def along_z(t):
        m = (0, 1) if t == last else (None, None)
        first, second = (0, 0) if t == 1 else (2 * t - 3, 2 * t - 2)
        here = block(x, c, first, m[0])
        start(remote(here, here, ws.at[0, t], wr.at[0, t], up))
        here = block(x, c, second, m[1])
        start(remote(here, here, ws.at[1, t], wr.at[1, t], down))

    def from_z(t):
        first, second = (2 * t - 1, 2 * t) if t < last else (NZ - 1, NZ - 1)
        m = (0, 1) if t == last else (None, None)
        here = block(x, c, first, m[0])
        remote(here, here, ws.at[0, t], wr.at[0, t], sib).wait_recv()
        here = block(x, c, second, m[1])
        remote(here, here, ws.at[1, t], wr.at[1, t], sib).wait_recv()

    def spread_x(k):
        here = block(x, c, k)
        start(remote(here, here, xs.at[0, k], xr.at[0, k], right))
        start(remote(here, here, xs.at[1, k], xr.at[1, k], left))
        start(remote(here, here, cs.at[0, k], cr.at[0, k], sib))

    def from_x(k):
        here = block(xl, c, k)
        remote(here, here, xs.at[0, k], xr.at[0, k], sib).wait_recv()
        half = block(xl, c, k, 0)
        start(remote(half, half, xs.at[2, k], xr.at[2, k], right))
        start(remote(here, here, cs.at[1, k], cr.at[1, k], sib))
        here = block(xr_, c, k)
        remote(here, here, xs.at[1, k], xr.at[1, k], sib).wait_recv()
        half = block(xr_, c, k, 1)
        start(remote(half, half, xs.at[3, k], xr.at[3, k], left))
        start(remote(here, here, cs.at[2, k], cr.at[2, k], sib))

    def from_two(k):
        for m in range(2):
            half = block(xo, c, k, m)
            remote(half, half, xs.at[2 + m, k], xr.at[2 + m, k], sib).wait_recv()
        here = block(xo, c, k)
        start(remote(here, here, cs.at[3, k], cr.at[3, k], sib))

    def other_core(i, at_x):
        for k in range(NZ):
            here = block(at_x, 1 - c, k)
            remote(here, here, cs.at[i, k], cr.at[i, k], sib).wait_recv()

    @pl.when(holder)
    def _():
        w_own.wait()

    @pl.when(jnp.logical_not(holder))
    def _():
        here = wbuf.at[:, spot(x, c), zcols]
        remote(here, here, ws.at[0, 0], wr.at[0, 0], sib).wait_recv()

    along_z(1)
    spread_x(0)
    for t in range(1, last):
        from_z(t)
        along_z(t + 1)
        spread_x(2 * t - 1)
        spread_x(2 * t)
        for n in ((0,) if t == 1 else (2 * t - 3, 2 * t - 2)):
            from_x(n)
    from_z(last)
    spread_x(NZ - 1)

    token_spot = rows(s * BLOCK, BLOCK)
    qkv_copies = []
    for i, (src, dst) in enumerate(((q, qh), (k, kh), (v, vh))):
        cp = pltpu.make_async_copy(src.at[:, lanes(s * HD, HD)], dst.at[token_spot], loc.at[2 + i])
        cp.start()
        qkv_copies.append(cp)
    for p in range(1, NS):
        to = lax.rem(s + p, NS)
        for i, (src, dst) in enumerate(((q, qh), (k, kh), (v, vh))):
            cp = remote(
                src.at[:, lanes(to * HD, HD)], dst.at[token_spot],
                qs.at[i, p], qr.at[i, p], device(x, y, to),
            )
            cp.start()
            qkv_copies.append(cp)

    go_own.wait()
    for cp in go_copies:
        cp.wait()
    gog_own = pltpu.make_async_copy(gobuf, gog.at[x], loc.at[5])
    gog_own.start()
    for d in range(1, NY):
        here = mbuf.at[x * NY + lax.rem(y + NY - d, NY)]
        mask_copies[d - 1].wait_send()
        remote(here, here, ms.at[d], mr.at[d], sib).wait_recv()
    mask_copies = []
    for a in range(1, NX):
        here = mbuf.at[pl.ds(x * NY, NY)]
        cp = remote(here, here, ms.at[NY + a], mr.at[NY + a], device(lax.rem(x + a, NX), y, s))
        cp.start()
        mask_copies.append(cp)
    for b in range(NY):
        one = mbuf[x * NY + b, 0:1, :]
        zero = (1.0 - one.astype(F32)).astype(BF)
        for j in range(NZ):
            piece = gobuf[b, :, j * 128 : (j + 1) * 128]
            gom[0, b * BLOCK : (b + 1) * BLOCK, j * 128 : (j + 1) * 128] = piece * zero
            gom[1, b * BLOCK : (b + 1) * BLOCK, j * 128 : (j + 1) * 128] = piece * one
    y_copies = {}

    def compute(step, at_x, at_c):
        f = at_x * 2 + at_c
        part_rows = spot(at_x, at_c)
        cols = lanes(f * fc, fc)
        acc = lax.dot_general(
            gom[0], wbuf[0, part_rows, :], (((1,), (1,)), ((), ())), preferred_element_type=F32
        ) + lax.dot_general(
            gom[1], wbuf[1, part_rows, :], (((1,), (1,)), ((), ())), preferred_element_type=F32
        )
        low = acc.astype(BF)
        for b in range(NY):
            part[b, :, cols] = low[b * BLOCK : (b + 1) * BLOCK]
        y_copies[step] = []
        for d in range(1, NY):
            to = lax.rem(y + d, NY)
            cp = remote(
                part.at[to, :, cols], rsbuf.at[y, :, cols], ys.at[step, d], yr.at[step, d],
                device(x, to, s),
            )
            cp.start()
            y_copies[step].append(cp)

    def head_copies(at_x, at_c, h):
        f = at_x * 2 + at_c
        heads = fc // HD
        head = f * heads + h
        src = gasum.at[:, lanes(head * HD, HD)]
        far = remote(src, gah.at[token_spot], hs.at[head], hr.at[s], device(x, y, head))
        near = pltpu.make_async_copy(src, gah.at[token_spot], loc.at[6])
        return head, far, near

    def total(step, at_x, at_c):
        f = at_x * 2 + at_c
        cols = lanes(f * fc, fc)
        for cp in y_copies[step]:
            cp.wait()
        acc = part[y, :, cols].astype(F32)
        for d in range(1, NY):
            acc = acc + rsbuf[lax.rem(y + d, NY), :, cols].astype(F32)
        gasum[:, cols] = acc.astype(BF)
        for h in range(fc // HD):
            head, far, near = head_copies(at_x, at_c, h)

            @pl.when(head == s)
            def _():
                near.start()

            @pl.when(head != s)
            def _():
                far.start()

    order = [(x, c), (x, 1 - c), (xl, c), (xl, 1 - c), (xr_, c), (xr_, 1 - c), (xo, c), (xo, 1 - c)]
    from_two(0)
    compute(0, *order[0])
    for n in (NZ - 3, NZ - 2):
        from_x(n)
    for n in (1, 2):
        from_two(n)
    other_core(0, x)
    compute(1, *order[1])
    from_x(NZ - 1)
    total(0, *order[0])
    compute(2, *order[2])
    for n in (3, 4):
        from_two(n)
    compute(4, *order[4])
    total(1, *order[1])
    other_core(1, xl)
    compute(3, *order[3])
    total(2, *order[2])
    other_core(2, xr_)
    compute(5, *order[5])
    total(4, *order[4])
    for n in (5, 6, 7):
        from_two(n)
    total(3, *order[3])
    total(5, *order[5])

    gog_own.wait()
    go_right = remote(gobuf, gog.at[x], os.at[0], orr.at[0], right)
    go_left = remote(gobuf, gog.at[x], os.at[1], orr.at[1], left)
    go_right.start()
    go_left.start()

    compute(6, *order[6])
    other_core(3, xo)
    compute(7, *order[7])
    keep = pltpu.make_async_copy(wbuf, wg, loc.at[7])
    keep.start()
    total(6, *order[6])
    total(7, *order[7])

    for step in range(8):
        for h in range(fc // HD):
            head, far, near = head_copies(*order[step], h)

            @pl.when(head == s)
            def _():
                near.wait()

            @pl.when(head != s)
            def _():
                far.wait_send()

    for p in range(1, NS):
        src = lax.rem(s + NS - p, NS)
        here = gah.at[rows(src * BLOCK, BLOCK)]
        remote(here, here, hs.at[0], hr.at[src], sib).wait_recv()
    for cp in qkv_copies:
        cp.wait()

    @pl.when(holder)
    def _():
        w_sib.wait_send()

    for cp in sent:
        cp.wait_send()
    for a in range(1, NX):
        here = mbuf.at[pl.ds(lax.rem(x + NX - a, NX) * NY, NY)]
        mask_copies[a - 1].wait_send()
        remote(here, here, ms.at[NY + a], mr.at[NY + a], sib).wait_recv()
    masks[...] = mbuf[...]
    go_right.wait()
    go_left.wait()
    keep.wait()


def attend_kernel(
    mod, q_in, k_in, v_in, ga_in, att_out, dq_out, dk_out, dv_out,
    end, s_buf, dk_t, dv_t, q, k, v, ga, att, dq, dk, dv, ins, outs,
):
    length = q.shape[0]
    loads = []
    for i, (src, dst) in enumerate(((q_in, q), (k_in, k), (v_in, v), (ga_in, ga))):
        cp = pltpu.make_async_copy(src, dst, ins.at[i])
        cp.start()
        loads.append(cp)
    stores = []

    def store(i, src, dst, at):
        cp = pltpu.make_async_copy(src.at[at], dst.at[at], outs.at[i, at.start // at.size])
        cp.start()
        stores.append(cp)

    blocks = length // BLOCK
    qb = 4 * BLOCK
    kb = 2 * BLOCK
    strips = length // qb
    scale = HD ** -0.5
    c2 = scale * math.log2(math.e)
    end[blocks - 1] = length
    for b in range(blocks - 2, -1, -1):
        end[b] = jnp.where(mod[0, b + 1] == 1, end[b + 1], (b + 1) * BLOCK)
    dk_t[...] = jnp.zeros_like(dk_t)
    dv_t[...] = jnp.zeros_like(dv_t)
    nt = (((1,), (1,)), ((), ()))
    row = lax.broadcasted_iota(jnp.int32, (qb, 1), 0)

    loads[0].wait()
    loads[1].wait()
    for i in range(strips):
        q_rows = pl.ds(i * qb, qb)
        buf = s_buf.at[i % 2]
        qi = q[q_rows, :]
        limit, most = row + (i * qb + 1), (i + 1) * qb
        for b in range(qb // BLOCK):
            at = i * (qb // BLOCK) + b
            reach = jnp.where(mod[0, at] == 1, end[at], 0)
            most = jnp.maximum(most, reach)
            inside = jnp.logical_and(row >= b * BLOCK, row < (b + 1) * BLOCK)
            limit = jnp.where(inside, jnp.maximum(limit, reach), limit)
        fixed = -(-(i + 1) * qb // kb)
        n = lax.div(most + (kb - 1), kb)

        def part(j):
            return pl.ds(j * kb if isinstance(j, int) else pl.multiple_of(j * kb, kb), kb)

        def chunks(body, carry):
            for j in range(fixed):
                carry = body(j, carry)
            if fixed * kb < length:
                carry = lax.fori_loop(fixed, n, body, carry)
            return carry

        def scores(j, m):
            sc = lax.dot_general(qi, k[part(j), :], nt, preferred_element_type=F32)
            if not isinstance(j, int) or (j + 1) * kb > i * qb:
                col = lax.broadcasted_iota(jnp.int32, (qb, kb), 1) + j * kb
                sc = jnp.where(col < limit, sc, NEG)
            buf[j] = sc
            for t in range(kb // 128):
                m = jnp.maximum(m, sc[:, t * 128 : (t + 1) * 128])
            return m

        m = chunks(scores, jnp.full((qb, 128), NEG, F32))
        m = jnp.max(m, axis=1, keepdims=True)

        if i == 0:
            loads[2].wait()
            loads[3].wait()
        gi = ga[q_rows, :].astype(F32)

        def forward(j, carry):
            total, acc = carry
            e = jnp.exp2((buf[j] - m) * c2)
            buf[j] = e
            for t in range(kb // 128):
                total = total + e[:, t * 128 : (t + 1) * 128]
            return total, acc + jnp.dot(e.astype(BF), v[part(j), :], preferred_element_type=F32)

        total, acc = chunks(forward, (jnp.zeros((qb, 128), F32), jnp.zeros((qb, HD), F32)))
        inv = 1.0 / jnp.sum(total, axis=1, keepdims=True)
        out = (acc * inv).astype(BF)
        att[q_rows, :] = out
        store(0, att, att_out, q_rows)
        gl = gi * inv
        delta = jnp.sum(gl * out.astype(F32), axis=1, keepdims=True)
        gl = gl.astype(BF)
        gt = gl.T
        qt = qi.T

        def backward(j, acc):
            e = buf[j]
            dp = lax.dot_general(gl, v[part(j), :], nt, preferred_element_type=F32)
            ds = (e * (dp - delta)).astype(BF)
            dv_t[:, part(j)] += jnp.dot(gt, e.astype(BF), preferred_element_type=F32)
            dk_t[:, part(j)] += jnp.dot(qt, ds, preferred_element_type=F32)
            return acc + jnp.dot(ds, k[part(j), :], preferred_element_type=F32)

        acc = chunks(backward, jnp.zeros((qb, HD), F32))
        dq[q_rows, :] = (acc * scale).astype(BF)
        store(1, dq, dq_out, q_rows)

    for i in range(strips):
        spot = pl.ds(i * qb, qb)
        dk[spot, :] = (dk_t[:, spot].T * scale).astype(BF)
        dv[spot, :] = dv_t[:, spot].T.astype(BF)
        store(2, dk, dk_out, spot)
        store(3, dv, dv_out, spot)
    for cp in stores:
        cp.wait()


def project_kernel(
    att, dq, dk, dv, wg, gog, masks,
    mixo, dqo, dko, dvo, gwo,
    aall, gatt, wv, gov, am, gm, mixp, gws, gwr, gwz, zbuf, fin,
    loc, hs, hr, ps, pr, ys, yr, qs, qr, xs, xr, cs, cr, zs, zr, fs_, fr, os, orr,
):
    x, y, z, c, s = place()
    width = wg.shape[1]
    fs = width // NX
    fc = fs // 2
    cols = wg.shape[2]
    tokens = NX * NY * BLOCK
    enter(x, y, z, c, s, True)
    sib = device(x, y, 2 * z + 1 - c)

    head_spot = lanes(s * HD, HD)
    a_own = pltpu.make_async_copy(att.at[rows(s * BLOCK, BLOCK)], aall.at[y, :, head_spot], loc.at[0])
    a_own.start()
    a_copies = []
    for p in range(1, NS):
        to = lax.rem(s + p, NS)
        cp = remote(
            att.at[rows(to * BLOCK, BLOCK)], aall.at[y, :, head_spot], hs.at[p], hr.at[p],
            device(x, y, to),
        )
        cp.start()
        a_copies.append(cp)
    xl, xo, xr_ = lax.rem(x + NX - 1, NX), lax.rem(x + 2, NX), lax.rem(x + 1, NX)
    left, right = device(xl, y, s), device(xr_, y, s)
    half = HALF * BLOCK

    def go_part(at_x, h):
        return pl.ds(pl.multiple_of(at_x * (NY * BLOCK) + h * half, half), half)

    on_right = remote(gog.at[go_part(xl, 0)], gov.at[go_part(xl, 0)], os.at[0], orr.at[0], right)
    on_left = remote(gog.at[go_part(xr_, 1)], gov.at[go_part(xr_, 1)], os.at[1], orr.at[1], left)
    on_right.start()
    on_left.start()
    load_go = []
    for i, at_x in enumerate((x, xl, xr_)):
        spot = pl.ds(pl.multiple_of(at_x * (NY * BLOCK), NY * BLOCK), NY * BLOCK)
        cp = pltpu.make_async_copy(gog.at[spot], gov.at[spot], loc.at[8 + i])
        cp.start()
        load_go.append(cp)
    load_w = pltpu.make_async_copy(wg, wv, loc.at[2])
    load_w.start()
    a_own.wait()
    for cp in a_copies:
        cp.wait()

    def y_copy(block, d, a):
        spot = aall.at[block, :, lanes(lax.rem(x + a, NX) * fs, fs)]
        return remote(spot, spot, ys.at[d, a], yr.at[d, a], device(x, lax.rem(y + d, NY), s))

    def x_copy(block, d, a):
        to_x = lax.rem(x + a, NX)
        return remote(
            aall.at[block, :, lanes(to_x * fs, fs)], gatt.at[x * NY + block],
            ps.at[d, a], pr.at[d, a], device(to_x, y, s),
        )

    for a in (2, 1, 3):
        for d in (1, 3, 2):
            y_copy(y, d, a).start()
        x_copy(y, 0, a).start()
    for d in (1, 3, 2):
        y_copy(y, d, 0).start()
    q_copies = []
    for i, (src, dst) in enumerate(((dq, dqo), (dk, dko), (dv, dvo))):
        cp = pltpu.make_async_copy(src.at[rows(s * BLOCK, BLOCK)], dst.at[:, head_spot], loc.at[3 + i])
        cp.start()
        q_copies.append(cp)
    for p in range(1, NS):
        to = lax.rem(s + p, NS)
        for i, (src, dst) in enumerate(((dq, dqo), (dk, dko), (dv, dvo))):
            cp = remote(
                src.at[rows(to * BLOCK, BLOCK)], dst.at[:, head_spot], qs.at[i, p], qr.at[i, p],
                device(x, y, to),
            )
            cp.start()
            q_copies.append(cp)

    for a in (2, 1, 3, 0):
        for d in (1, 3, 2):
            y_copy(y, d, a).wait_send()
            src = lax.rem(y + NY - d, NY)
            spot = aall.at[src, :, lanes(lax.rem(x + a, NX) * fs, fs)]
            remote(spot, spot, ys.at[d, a], yr.at[d, a], sib).wait_recv()
            if a:
                x_copy(src, d, a).start()
    for b in range(NY):
        gatt[x * NY + b] = aall[b, :, lanes(x * fs, fs)]

    step = 256
    pairs = cols // step

    for a in range(1, NX):
        for d in range(NY):
            x_copy(lax.rem(y + NY - d, NY), d, a).wait_send()
            block = gatt.at[lax.rem(x + NX - a, NX) * NY + lax.rem(y + NY - d, NY)]
            remote(block, block, ps.at[d, a], pr.at[d, a], sib).wait_recv()

    def spread(t, carry):
        one = masks[t, 0:1, :]
        zero = (1.0 - one.astype(F32)).astype(BF)
        spot = pl.ds(pl.multiple_of(t * BLOCK, BLOCK), BLOCK)
        for j in range(fs // 128):
            piece = gatt[t, :, j * 128 : (j + 1) * 128].T
            gm[j * 128 : (j + 1) * 128, spot] = piece * zero
            gm[fs + j * 128 : fs + (j + 1) * 128, spot] = piece * one
        return carry

    lax.fori_loop(0, NX * NY, spread, 0)
    for cp in load_go:
        cp.wait()
    on_right.wait()
    on_left.wait()

    def theirs(t, carry):
        spot = pl.ds(pl.multiple_of(lax.rem(lax.div(z, 2) + 1 + t, pairs) * step, step), step)
        for m in range(2):
            lhs = gm[rows(m * fs + (1 - c) * fc, fc), :]
            gws[m, :, spot] = jnp.dot(lhs, gov[:, spot], preferred_element_type=F32).astype(BF)
        remote(gws.at[:, :, spot], gwr.at[:, :, spot], cs.at[t], cr.at[t], sib).start()
        return carry

    def to_plane(i):
        return remote(gwz.at[i], zbuf.at[z], zs.at[i], zr.at[z], device(x, y, 2 * i + c))

    def ours(t, carry):
        pair = lax.rem(lax.div(z, 2) + 1 + t, pairs)
        spot = pl.ds(pl.multiple_of(pair * step, step), step)
        own = []
        for m in range(2):
            lhs = gm[rows(m * fs + c * fc, fc), :]
            own.append(jnp.dot(lhs, gov[:, spot], preferred_element_type=F32))
        remote(gws.at[:, :, spot], gwr.at[:, :, spot], cs.at[t], cr.at[t], sib).wait()
        for m in range(2):
            low = (own[m] + gwr[m, :, spot].astype(F32)).astype(BF)
            for i in range(2):
                gwz[2 * pair + i, m] = low[:, i * 128 : (i + 1) * 128]
        for i in range(2):
            @pl.when(2 * pair + i != z)
            def _():
                to_plane(2 * pair + i).start()
        return carry

    def both(t, carry):
        @pl.when(t < pairs)
        def _():
            theirs(t, 0)

        @pl.when(t > 0)
        def _():
            ours(t - 1, 0)

        return carry

    lax.fori_loop(0, pairs + 1, both, 0)
    for b in range(NY):
        one = masks[x * NY + b, 0:1, :]
        zero = (1.0 - one.astype(F32)).astype(BF)
        for j in range(width // 128):
            piece = aall[b, :, j * 128 : (j + 1) * 128]
            am[0, b * BLOCK : (b + 1) * BLOCK, j * 128 : (j + 1) * 128] = piece * zero
            am[1, b * BLOCK : (b + 1) * BLOCK, j * 128 : (j + 1) * 128] = piece * one
    load_w.wait()

    def mix_copy(i, d):
        to = lax.rem(y + d, NY)
        return remote(
            mixp.at[to, :, lanes(i * 128, 128)], mixo.at[:, lanes((i * NY + y) * 128, 128)],
            xs.at[d], xr.at[d], device(x, to, s),
        )

    def mix(t, carry):
        spot = pl.ds(pl.multiple_of(t * step, step), step)
        acc = jnp.dot(am[0], wv[0, :, spot], preferred_element_type=F32)
        acc = acc + jnp.dot(am[1], wv[1, :, spot], preferred_element_type=F32)
        low = acc.astype(BF)
        for b in range(NY):
            mixp[b, :, spot] = low[b * BLOCK : (b + 1) * BLOCK]
        for d in range(1, NY):
            for i in range(step // 128):
                mix_copy(t * (step // 128) + i, d).start()
        return carry

    lax.fori_loop(0, cols // step, mix, 0)
    m_copies = []
    for d in range(1, NY):
        to = lax.rem(y + d, NY)
        m_copies.append(remote(mixp.at[to], mixp.at[to], xs.at[d], xr.at[d], device(x, to, s)))
    for i in range(NZ):
        pltpu.make_async_copy(
            mixp.at[y, :, pl.ds(i * 128, 128)], mixo.at[:, lanes((i * NY + y) * 128, 128)], loc.at[6]
        ).start()
    m_own = pltpu.make_async_copy(mixp.at[y], mixp.at[y], loc.at[6])

    for d in range(1, NZ):
        to_plane(lax.rem(z + d, NZ)).wait_send()
        src = lax.rem(z + NZ - d, NZ)
        remote(gwz.at[0], zbuf.at[src], zs.at[0], zr.at[src], sib).wait_recv()
    for m in range(2):
        acc = gwz[z, m].astype(F32)
        for d in range(1, NZ):
            acc = acc + zbuf[lax.rem(z + d, NZ), m].astype(F32)
        for j in range(HALF):
            fin[j, m] = acc[j * 128 : (j + 1) * 128]
    spot = lanes(lax.rem(y, HALF) * 128, 128)
    for j in range(HALF):
        to_y = c * HALF + j
        to_c = lax.div(y, HALF)
        here = jnp.logical_and(to_y == y, to_c == c)
        near = pltpu.make_async_copy(fin.at[j], gwo.at[:, :, spot], loc.at[7])
        far = remote(
            fin.at[j], gwo.at[:, :, spot], fs_.at[j], fr.at[lax.rem(y, HALF)],
            device(x, to_y, 2 * z + to_c),
        )

        @pl.when(here)
        def _():
            near.start()
            near.wait()

        @pl.when(jnp.logical_not(here))
        def _():
            far.start()
            far.wait_send()

    for i in range(HALF):
        from_y = c * HALF + i
        from_c = lax.div(y, HALF)
        here = jnp.logical_and(from_y == y, from_c == c)

        @pl.when(jnp.logical_not(here))
        def _():
            place_ = gwo.at[:, :, pl.ds(i * 128, 128)]
            remote(fin.at[0], place_, fs_.at[0], fr.at[i], sib).wait_recv()

    m_own.wait()
    for cp in m_copies + q_copies:
        cp.wait()


def hbm(n):
    return [pl.BlockSpec(memory_space=pltpu.HBM)] * n


def local(queries, keys, values, w_out, modality, grad_out):
    dma = pltpu.SemaphoreType.DMA
    tokens = queries.shape[1]
    width = queries.shape[2]
    length = tokens * NS
    group = NZ * 128
    shape = jax.ShapeDtypeStruct
    vmem = pl.BlockSpec(memory_space=pltpu.VMEM)
    smem = pl.BlockSpec(memory_space=pltpu.SMEM)
    head = shape((length, HD), BF)
    qh, kh, vh, gah, wg, gog, masks = pl.pallas_call(
        gather_kernel,
        out_shape=(
            head, head, head, head,
            shape((2, width, group), BF),
            shape((NX, NY, BLOCK, group), BF),
            shape((NX * NY, 16, 128), BF),
        ),
        in_specs=[smem] + hbm(5),
        out_specs=tuple(hbm(6) + [vmem]),
        scratch_shapes=[
            pltpu.VMEM((2, width, group), BF),
            pltpu.VMEM((NY, BLOCK, group), BF),
            pltpu.VMEM((2, NY * BLOCK, group), BF),
            pltpu.VMEM((NY, BLOCK, width), BF),
            pltpu.VMEM((NY, BLOCK, width), BF),
            pltpu.VMEM((BLOCK, width), BF),
            pltpu.VMEM((NX * NY, 16, 128), BF),
            dma((8,)),
            dma((3, NS)), dma((3, NS)),
            dma((2, NZ)), dma((2, NZ)),
            dma((4, NZ)), dma((4, NZ)),
            dma((4, NZ)), dma((4, NZ)),
            dma((NY,)), dma((NY,)),
            dma((NX * NY,)), dma((NX * NY,)),
            dma((8, NY)), dma((8, NY)),
            dma((NS,)), dma((NS,)),
            dma((2,)), dma((2,)),
        ],
        compiler_params=pltpu.CompilerParams(
            collective_id=0, has_side_effects=True, vmem_limit_bytes=40 << 20
        ),
        name="gather",
    )(modality, queries[0], keys[0], values[0], w_out, grad_out[0])

    att, dq, dk, dv = pl.pallas_call(
        attend_kernel,
        out_shape=(head, head, head, head),
        in_specs=[smem] + hbm(4),
        out_specs=tuple(hbm(4)),
        scratch_shapes=[
            pltpu.SMEM((length // BLOCK,), jnp.int32),
            pltpu.VMEM((2, length // 256, 512, 256), F32),
            pltpu.VMEM((HD, length), F32),
            pltpu.VMEM((HD, length), F32),
        ]
        + [pltpu.VMEM((length, HD), BF)] * 8
        + [dma((4,)), dma((4, length // 256))],
        compiler_params=pltpu.CompilerParams(vmem_limit_bytes=40 << 20),
        name="attend",
    )(modality, qh, kh, vh, gah)

    fs = width // NX
    all_tokens = NX * NY * BLOCK
    flat = shape((tokens, width), BF)
    mixo, dqo, dko, dvo, gwo = pl.pallas_call(
        project_kernel,
        out_shape=(
            shape((tokens, NY * group), BF), flat, flat, flat,
            shape((2, 128, HALF * 128), F32),
        ),
        in_specs=hbm(6) + [vmem],
        out_specs=tuple(hbm(5)),
        scratch_shapes=[
            pltpu.VMEM((NY, BLOCK, width), BF),
            pltpu.VMEM((NX * NY, BLOCK, fs), BF),
            pltpu.VMEM((2, width, group), BF),
            pltpu.VMEM((all_tokens, group), BF),
            pltpu.VMEM((2, NY * BLOCK, width), BF),
            pltpu.VMEM((2 * fs, all_tokens), BF),
            pltpu.VMEM((NY, BLOCK, group), BF),
            pltpu.VMEM((2, fs // 2, group), BF),
            pltpu.VMEM((2, fs // 2, group), BF),
            pltpu.VMEM((NZ, 2, fs // 2, 128), BF),
            pltpu.VMEM((NZ, 2, fs // 2, 128), BF),
            pltpu.VMEM((HALF, 2, 128, 128), F32),
            dma((11,)),
            dma((NS,)), dma((NS,)),
            dma((NY, NX)), dma((NY, NX)),
            dma((NY, NX)), dma((NY, NX)),
            dma((3, NS)), dma((3, NS)),
            dma((NY,)), dma((NY,)),
            dma((group // 256,)), dma((group // 256,)),
            dma((NZ,)), dma((NZ,)),
            dma((HALF,)), dma((HALF,)),
            dma((2,)), dma((2,)),
        ],
        compiler_params=pltpu.CompilerParams(
            collective_id=1, has_side_effects=True, vmem_limit_bytes=52 << 20
        ),
        name="project",
    )(att, dq, dk, dv, wg, gog.reshape(all_tokens, group), masks)
    return mixo[None], dqo[None], dko[None], dvo[None], gwo


def solution(mesh):
    return jax.shard_map(
        local,
        mesh=mesh,
        in_specs=(
            P("dp", "seq", None),
            P("dp", "seq", None),
            P("dp", "seq", None),
            P(None, None, "seq"),
            P("dp", None),
            P("dp", "seq", None),
        ),
        out_specs=(
            P("dp", "seq", None),
            P("dp", "seq", None),
            P("dp", "seq", None),
            P("dp", "seq", None),
            P(None, "dp", "seq"),
        ),
        check_vma=False,
    )
```
